32 devices in a mesh: dp: 8 (over z, x), seq: 4 (over y, core).
Axes of the slice: x: 2, y: 2, z: 4, core: 2. Of those that a mesh axis runs over, the one named last changes fastest.
Arguments:
- tokens: bfloat16 [16, 1024, 1536], P('dp', 'seq'), may hold values from -6 to 6
- cotangent: bfloat16 [16, 1024, 1536], P('dp', 'seq'), may hold values from -6 to 6
- attn_norm: bfloat16 [2, 1536], P(None, 'dp'), may hold values from 0.5 to 1.5
- w_query: bfloat16 [2, 1536, 1536], P(None, 'dp'), may hold values from -0.15625 to 0.15625
- w_key: bfloat16 [2, 1536, 768], P(None, 'dp'), may hold values from -0.15625 to 0.15625
- w_value: bfloat16 [2, 1536, 768], P(None, 'dp'), may hold values from -0.15625 to 0.15625
- w_out: bfloat16 [2, 1536, 1536], P(None, 'dp'), may hold values from -0.875 to 0.875
- mlp_norm: bfloat16 [2, 1536], P(None, 'dp'), may hold values from 0.5 to 1.5
- w_gate: bfloat16 [2, 1536, 4096], P(None, 'dp'), may hold values from -0.15625 to 0.15625
- w_up: bfloat16 [2, 1536, 4096], P(None, 'dp'), may hold values from -0.15625 to 0.15625
- w_down: bfloat16 [2, 4096, 1536], P(None, 'dp'), may hold values from -0.125 to 0.125
Outputs:
- out: bfloat16 [16, 1024, 1536], P('dp', 'seq')
- d_tokens: float32 [16, 1024, 1536], P('dp', 'seq')
- grad_attn_norm: float32 [2, 1536], P(None, 'dp')
- grad_w_query: float32 [2, 1536, 1536], P(None, 'dp')
- grad_w_key: float32 [2, 1536, 768], P(None, 'dp')
- grad_w_value: float32 [2, 1536, 768], P(None, 'dp')
- grad_w_out: float32 [2, 1536, 1536], P(None, 'dp')
- grad_mlp_norm: float32 [2, 1536], P(None, 'dp')
- grad_w_gate: float32 [2, 1536, 4096], P(None, 'dp')
- grad_w_up: float32 [2, 1536, 4096], P(None, 'dp')
- grad_w_down: float32 [2, 4096, 1536], P(None, 'dp')
The draws below stay inside these ranges and needn't reach their ends.
All inputs are finite; a program needn't handle non-finite values.
Results may differ from the reference program's by a relative error of at most 0.029.
Values may be sent and summed in bfloat16 or wider, within the bound.
No kernel may reach another device: no remote copies, remote signals or barrier semaphores. Data moves between devices by JAX's collectives and lax.ppermute only.
A program may use at most 448 MiB of HBM per device.

```python
import math
import jax
import jax.numpy as jnp
from jax import lax

D = 1536
QH = 16
KVH = 8
HD = 96
FF = 4096
LAYERS = 2
LEN = 1024
SEQS = 16


def shard_levels(key, dims, split, smallest, high):
    level = 1.0
    for axis_at, parts in split:
        steps = jax.random.uniform(jax.random.fold_in(jax.random.fold_in(key, 6), axis_at), (parts,), jnp.float32, smallest / len(split), high / len(split))
        level = level * jnp.repeat(jnp.exp(steps), dims[axis_at] // parts).reshape((-1,) + (1,) * (len(dims) - 1 - axis_at))
    return level


def centred(own_key, dims, spread, limit, cuts=(), held_as=jnp.bfloat16):
    values = spread * jax.random.normal(own_key, dims, jnp.float32)
    if cuts:
        values = values * shard_levels(own_key, dims, cuts, -0.22, 0.18)
    return jnp.clip(values, -limit, limit).astype(held_as)


def setup_inputs(seed: int = 0) -> dict:
    key_list = jax.random.split(jax.random.key(seed), 12)
    tokens = centred(key_list[0], (SEQS, LEN, D), 1.0, 6.0, ((0, 8), (1, 4)))
    cotangent = centred(key_list[1], (SEQS, LEN, D), 1.0, 6.0, ((0, 8), (1, 4)))
    attn_norm = jnp.clip(1.0 + 0.1 * jax.random.normal(key_list[2], (LAYERS, D), jnp.float32), 0.5, 1.5).astype(jnp.bfloat16)
    w_query = centred(key_list[3], (LAYERS, D, D), D ** -0.5, 0.15625, ((1, 8),))
    w_key = centred(key_list[4], (LAYERS, D, KVH * HD), D ** -0.5, 0.15625, ((1, 8),))
    w_value = centred(key_list[5], (LAYERS, D, KVH * HD), D ** -0.5, 0.15625, ((1, 8),))
    w_out = centred(key_list[6], (LAYERS, D, D), (D // 32) ** -0.5, 0.875, ((1, 8),))
    mlp_norm = jnp.clip(1.0 + 0.1 * jax.random.normal(key_list[7], (LAYERS, D), jnp.float32), 0.5, 1.5).astype(jnp.bfloat16)
    w_gate = centred(key_list[8], (LAYERS, D, FF), D ** -0.5, 0.15625, ((1, 8),))
    w_up = centred(key_list[9], (LAYERS, D, FF), D ** -0.5, 0.15625, ((1, 8),))
    w_down = centred(key_list[10], (LAYERS, FF, D), (FF // 2) ** -0.5, 0.125, ((1, 8),))
    return {"tokens": tokens, "cotangent": cotangent, "attn_norm": attn_norm, "w_query": w_query, "w_key": w_key, "w_value": w_value, "w_out": w_out, "mlp_norm": mlp_norm, "w_gate": w_gate, "w_up": w_up, "w_down": w_down}


epsilon = 1e-05
rope_base = 100000.0
HIGHEST = lax.Precision.HIGHEST

@jax.custom_vjp
def low(v):
    return lax.optimization_barrier(v.astype(jnp.bfloat16)).astype(jnp.float32)

@jax.custom_vjp
def low_back(v):
    return v

def low_keep(v):
    return (low(v), None)

def low_pass(kept, grad):
    return (grad,)

def back_keep(v):
    return (v, None)

def back_low(kept, grad):
    return (low(grad),)
low.defvjp(low_keep, low_pass)
low_back.defvjp(back_keep, back_low)

def rotate(values, cosine, sine):
    middle = values.shape[-1] // 2
    first = values[..., :middle]
    second = values[..., middle:]
    cos_b = cosine[:, None, :]
    sin_b = sine[:, None, :]
    return jnp.concatenate([first * cos_b - second * sin_b, second * cos_b + first * sin_b], axis=-1)

def rms_norm(stream, gain):
    inverse = lax.rsqrt(lax.optimization_barrier(jnp.mean(stream * stream, axis=-1, keepdims=True)) + epsilon)
    return stream * inverse * gain

def attention_one(pieces):
    queries, keys, values = pieces
    length = queries.shape[0]
    grouped = queries.reshape(length, KVH, 2, HD)
    raw = jnp.einsum('qgah,kgh->gaqk', grouped, keys, precision=HIGHEST) * HD ** (-0.5)
    causal = jnp.arange(length)[:, None] >= jnp.arange(length)[None, :]
    scores = jnp.where(causal, low_back(raw), -1e+30)
    softened = low(jax.nn.softmax(scores, axis=-1))
    mixed = jnp.einsum('gaqk,kgh->qgah', softened, values, precision=HIGHEST)
    return low(low_back(mixed)).reshape(length, QH * HD)

def layer_ref(stream, params, cosine, sine):
    gain_one, query_weight, key_weight, value_weight, out_weight, gain_two, gate_weight, up_weight, down_weight = params
    group_size, length, features = stream.shape
    flat = stream.reshape(-1, features)
    input_one = low(rms_norm(flat, gain_one))
    query_raw = low_back(jnp.dot(input_one, query_weight, precision=HIGHEST))
    key_raw = low_back(jnp.dot(input_one, key_weight, precision=HIGHEST))
    value_raw = low(low_back(jnp.dot(input_one, value_weight, precision=HIGHEST)))
    queries = low(low_back(rotate(query_raw.reshape(group_size, length, QH, HD), cosine, sine)))
    keys = low(low_back(rotate(key_raw.reshape(group_size, length, KVH, HD), cosine, sine)))
    values = value_raw.reshape(group_size, length, KVH, HD)
    mixed = lax.map(jax.checkpoint(attention_one), (queries, keys, values)).reshape(-1, features)
    stream_two = flat + low_back(jnp.dot(mixed, out_weight, precision=HIGHEST))
    input_two = low(rms_norm(stream_two, gain_two))
    gate = low_back(jnp.dot(input_two, gate_weight, precision=HIGHEST))
    up_part = low_back(jnp.dot(input_two, up_weight, precision=HIGHEST))
    hidden = low(jax.nn.silu(gate) * up_part)
    result = stream_two + low_back(jnp.dot(hidden, down_weight, precision=HIGHEST))
    return result.reshape(group_size, length, features)

def reference(tokens, cotangent, attn_norm, w_query, w_key, w_value, w_out, mlp_norm, w_gate, w_up, w_down):
    float_params = tuple((item.astype(jnp.float32) for item in (attn_norm, w_query, w_key, w_value, w_out, mlp_norm, w_gate, w_up, w_down)))
    seq_total, length, features = tokens.shape
    group_size = math.gcd(seq_total, 4)
    block_count = seq_total // group_size
    middle = HD // 2
    frequency = rope_base ** (-jnp.arange(middle, dtype=jnp.float32) / middle)
    angles = jnp.arange(length, dtype=jnp.float32)[:, None] * frequency[None, :]
    cosine = jnp.cos(angles)
    sine = jnp.sin(angles)

    def forward(stream, params):
        for layer_idx in range(params[0].shape[0]):
            stream = layer_ref(stream, tuple((item[layer_idx] for item in params)), cosine, sine)
        return stream

    def scan_step(totals, pieces):
        block_rows, block_cot = pieces
        result, pullback = jax.vjp(forward, block_rows.astype(jnp.float32), float_params)
        grad_in, grad_params = pullback(block_cot.astype(jnp.float32))
        summed = tuple((left + right for left, right in zip(totals, grad_params)))
        return (summed, (result.astype(jnp.bfloat16), grad_in))
    initial = tuple((jnp.zeros(item.shape, jnp.float32) for item in float_params))
    totals, (outputs, grads) = lax.scan(scan_step, initial, (tokens.reshape(block_count, group_size, length, features), cotangent.reshape(block_count, group_size, length, features)))
    return (outputs.reshape(seq_total, length, features), grads.reshape(seq_total, length, features), totals[0], totals[1], totals[2], totals[3], totals[4], totals[5], totals[6], totals[7], totals[8])
```

```python
import jax
import jax.numpy as jnp
from jax import lax
from jax.sharding import PartitionSpec as P

HD = 96
SCALE = HD ** (-0.5)
EPSILON = 1e-05
ROPE_BASE = 100000.0

CORE_SWAP = [(0, 1), (1, 0), (2, 3), (3, 2)]
Y_SWAP = [(0, 2), (2, 0), (1, 3), (3, 1)]


def other_core(value):
    return lax.ppermute(value, "seq", CORE_SWAP)


def other_y(value):
    return lax.ppermute(value, "seq", Y_SWAP)


def gather_dp(piece):
    return lax.all_gather(piece, "dp", axis=0, tiled=True)


def scatter_dp(full):
    return lax.psum_scatter(full, "dp", scatter_dimension=0, tiled=True)


def dot(left, right):
    return jnp.dot(left, right, preferred_element_type=jnp.float32)


def dot_t(left, right):
    return lax.dot_general(
        left, right, (((1,), (1,)), ((), ())), preferred_element_type=jnp.float32
    )


def tdot(left, right):
    return lax.dot_general(
        left, right, (((0,), (0,)), ((), ())), preferred_element_type=jnp.float32
    )


def pair(flag, mine, other, axis=0):
    return jnp.where(
        flag == 0,
        jnp.concatenate([mine, other], axis=axis),
        jnp.concatenate([other, mine], axis=axis),
    )


def rotate(values, cosine, sine):
    middle = values.shape[-1] // 2
    first = values[..., :middle]
    second = values[..., middle:]
    cos_b = cosine[:, None, :]
    sin_b = sine[:, None, :]
    return jnp.concatenate(
        [first * cos_b - second * sin_b, second * cos_b + first * sin_b], axis=-1
    )


def norm_rows(stream, gain):
    inverse = lax.rsqrt(jnp.mean(stream * stream, axis=-1, keepdims=True) + EPSILON)
    normed = stream * inverse
    return (normed, inverse, (normed * gain).astype(jnp.bfloat16))


def norm_back(grad_out, normed, inverse, gain):
    gain_grad = jnp.sum(grad_out * normed, axis=0)
    scaled = grad_out * gain
    grad_in = inverse * (scaled - normed * jnp.mean(scaled * normed, axis=-1, keepdims=True))
    return (grad_in, gain_grad)


def scores_of(queries, keys, allowed):
    raw = jnp.einsum("qgah,kgh->gaqk", queries, keys, preferred_element_type=jnp.float32) * SCALE
    return jnp.where(allowed, raw, -1e30)


def attend_forward(queries, keys, values, allowed):
    scores = scores_of(queries, keys, allowed)
    maxima = jnp.max(scores, axis=-1, keepdims=True)
    exponent_vals = jnp.exp(scores - maxima)
    totals = jnp.sum(exponent_vals, axis=-1, keepdims=True)
    softened = (exponent_vals / totals).astype(jnp.bfloat16)
    mixed = jnp.einsum("gaqk,kgh->qgah", softened, values, preferred_element_type=jnp.float32)
    return (
        mixed.astype(jnp.bfloat16).reshape(mixed.shape[0], -1),
        (maxima + jnp.log(totals))[..., 0],
    )


def attend_backward(queries, keys, values, log_total, grad_out, allowed):
    scores = scores_of(queries, keys, allowed)
    softened = jnp.exp(scores - log_total[..., None])
    soft_low = softened.astype(jnp.bfloat16)
    grad_values = jnp.einsum(
        "gaqk,qgah->kgh", soft_low, grad_out, preferred_element_type=jnp.float32
    )
    grad_soft = jnp.einsum("qgah,kgh->gaqk", grad_out, values, preferred_element_type=jnp.float32)
    grad_scores = softened * (grad_soft - jnp.sum(softened * grad_soft, axis=-1, keepdims=True))
    scores_low = grad_scores.astype(jnp.bfloat16)
    grad_queries = (
        jnp.einsum("gaqk,kgh->qgah", scores_low, keys, preferred_element_type=jnp.float32) * SCALE
    )
    grad_keys = (
        jnp.einsum("gaqk,qgah->kgh", scores_low, queries, preferred_element_type=jnp.float32)
        * SCALE
    )
    return (
        grad_queries.astype(jnp.bfloat16),
        grad_keys.astype(jnp.bfloat16),
        grad_values.astype(jnp.bfloat16),
    )


def body(
    tokens, cotangent, attn_norm, w_query, w_key, w_value, w_out, mlp_norm, w_gate, w_up, w_down
):
    dp_size = lax.axis_size("dp")
    index = lax.axis_index("seq")
    core = index % 2
    side = index // 2
    _, span, features = tokens.shape
    layers = w_query.shape[0]
    rows = w_query.shape[1]
    q_half = w_query.shape[2] // 2
    k_half = w_key.shape[2] // 2
    ff = w_gate.shape[2]
    part = ff // (4 * dp_size)
    ff_quarter = ff // 4
    out_half = features // 2
    heads = q_half // HD
    kv_heads = k_half // HD
    mine_rows = 2 * span
    length = 4 * span

    def regroup(block):
        kept = lax.dynamic_index_in_dim(block, side, 0, keepdims=False)
        sent = lax.dynamic_index_in_dim(block, 1 - side, 0, keepdims=False)
        return pair(side, kept, other_y(sent))

    def ungroup(block):
        halves = block.reshape(2, span, features)
        kept = lax.dynamic_index_in_dim(halves, side, 0, keepdims=False)
        sent = lax.dynamic_index_in_dim(halves, 1 - side, 0, keepdims=False)
        got = other_y(sent)
        return pair(side, kept[None], got[None])

    def both_cores(value):
        return pair(core, value, other_core(value))

    def own_rows(total):
        kept = lax.dynamic_slice_in_dim(total, core * mine_rows, mine_rows, 0)
        sent = lax.dynamic_slice_in_dim(total, (1 - core) * mine_rows, mine_rows, 0)
        got = other_core(sent.astype(jnp.bfloat16))
        return kept + got.astype(jnp.float32)

    block_order = jnp.array([0, 2, 1, 3], jnp.int32)
    positions = (block_order[:, None] * span + jnp.arange(span)[None, :]).reshape(-1)
    middle = HD // 2
    frequency = ROPE_BASE ** (-jnp.arange(middle, dtype=jnp.float32) / middle)
    angles = positions.astype(jnp.float32)[:, None] * frequency[None, :]
    cosine = jnp.cos(angles)
    sine = jnp.sin(angles)
    allowed = positions[:, None] >= positions[None, :]

    gains = gather_dp(jnp.stack([attn_norm, mlp_norm]).reshape(2 * layers, rows).T)
    gains = gains.T.astype(jnp.float32).reshape(2, layers, features)

    def gather_layer(layer):
        qkv_local = jnp.concatenate(
            [
                lax.dynamic_slice_in_dim(w_query[layer], core * q_half, q_half, 1),
                lax.dynamic_slice_in_dim(w_key[layer], core * k_half, k_half, 1),
                lax.dynamic_slice_in_dim(w_value[layer], core * k_half, k_half, 1),
            ],
            axis=1,
        )
        qkv = gather_dp(qkv_local)
        out_cols = gather_dp(lax.dynamic_slice_in_dim(w_out[layer], core * out_half, out_half, 1))
        kept = lax.dynamic_slice_in_dim(out_cols, core * q_half, q_half, 0)
        sent = lax.dynamic_slice_in_dim(out_cols, (1 - core) * q_half, q_half, 0)
        out = pair(core, kept, other_core(sent), axis=1)

        def quarter(weight):
            cut = weight.reshape(rows, dp_size, 4, part)
            return lax.dynamic_index_in_dim(cut, index, 2, keepdims=False).reshape(rows, ff_quarter)

        gate_up = gather_dp(
            jnp.concatenate([quarter(w_gate[layer]), quarter(w_up[layer])], axis=1)
        )
        down = gather_dp(lax.dynamic_slice_in_dim(w_down[layer], index * part, part, 0))
        return qkv, out, ((gate_up, down), (other_y(gate_up), other_y(down)))

    def forward(stream, weights, gain_one, gain_two):
        qkv_w, out_w, mlp_w = weights
        normed_one, inverse_one, input_one = norm_rows(stream, gain_one)
        full_one = both_cores(input_one)
        raw = dot(full_one, qkv_w)
        queries = rotate(raw[:, :q_half].reshape(length, heads, HD), cosine, sine)
        keys = rotate(
            raw[:, q_half : q_half + k_half].reshape(length, kv_heads, HD), cosine, sine
        ).astype(jnp.bfloat16)
        queries = queries.astype(jnp.bfloat16).reshape(length, kv_heads, 2, HD)
        values = raw[:, q_half + k_half :].astype(jnp.bfloat16).reshape(length, kv_heads, HD)
        mixed, log_total = attend_forward(queries, keys, values, allowed)
        stream_two = stream + own_rows(dot(mixed, out_w))
        normed_two, inverse_two, input_two = norm_rows(stream_two, gain_two)
        full_two = both_cores(input_two)
        total = None
        kept_mlp = []
        for gate_up_w, down_w in mlp_w:
            gate_up = dot(full_two, gate_up_w)
            gate, up = gate_up[:, :ff_quarter], gate_up[:, ff_quarter:]
            hidden = (jax.nn.silu(gate) * up).astype(jnp.bfloat16)
            term = dot(hidden, down_w)
            total = term if total is None else total + term
            kept_mlp.append((gate, up, hidden))
        result = stream_two + own_rows(total)
        saved = (
            normed_one,
            inverse_one,
            full_one,
            queries,
            keys,
            values,
            log_total,
            mixed,
            normed_two,
            inverse_two,
            full_two,
            kept_mlp,
        )
        return result, saved

    def backward(grad, saved, weights, gain_one, gain_two):
        (
            normed_one,
            inverse_one,
            full_one,
            queries,
            keys,
            values,
            log_total,
            mixed,
            normed_two,
            inverse_two,
            full_two,
            kept_mlp,
        ) = saved
        qkv_w, out_w, mlp_w = weights
        grad_full = both_cores(grad.astype(jnp.bfloat16))
        total = None
        mlp_grads = []
        for (gate_up_w, down_w), (gate, up, hidden) in zip(mlp_w, kept_mlp):
            grad_down = tdot(hidden, grad_full).astype(jnp.bfloat16)
            grad_hidden = dot_t(grad_full, down_w)
            sig = jax.nn.sigmoid(gate)
            grad_gate = grad_hidden * up * sig * (1.0 + gate * (1.0 - sig))
            grad_up = grad_hidden * gate * sig
            grad_gate_up = jnp.concatenate([grad_gate, grad_up], axis=1).astype(jnp.bfloat16)
            grad_gate_up_w = tdot(full_two, grad_gate_up).astype(jnp.bfloat16)
            term = dot_t(grad_gate_up, gate_up_w)
            total = term if total is None else total + term
            mlp_grads.append((grad_gate_up_w, grad_down))
        grad_two = own_rows(total)
        norm_two_in, gain_two_g = norm_back(grad_two, normed_two, inverse_two, gain_two)
        grad_mid = grad + norm_two_in
        mid_full = both_cores(grad_mid.astype(jnp.bfloat16))
        grad_out_w = tdot(mixed, mid_full).astype(jnp.bfloat16)
        grad_mixed = dot_t(mid_full, out_w).astype(jnp.bfloat16)
        grad_heads = grad_mixed.reshape(length, kv_heads, 2, HD)
        grad_q, grad_k, grad_v = attend_backward(
            queries, keys, values, log_total, grad_heads, allowed
        )
        grad_q = rotate(
            grad_q.reshape(length, heads, HD).astype(jnp.float32), cosine, -sine
        ).astype(jnp.bfloat16)
        grad_k = rotate(grad_k.astype(jnp.float32), cosine, -sine).astype(jnp.bfloat16)
        grad_qkv = jnp.concatenate(
            [
                grad_q.reshape(length, q_half),
                grad_k.reshape(length, k_half),
                grad_v.reshape(length, k_half),
            ],
            axis=1,
        )
        grad_qkv_w = tdot(full_one, grad_qkv).astype(jnp.bfloat16)
        grad_one = own_rows(dot_t(grad_qkv, qkv_w))
        norm_one_in, gain_one_g = norm_back(grad_one, normed_one, inverse_one, gain_one)
        return grad_mid + norm_one_in, (mlp_grads, grad_out_w, grad_qkv_w, gain_one_g, gain_two_g)

    def seq_pieces(piece):
        cores = pair(core, piece[None], other_core(piece)[None])
        return pair(side, cores, other_y(cores))

    def reduce_mlp(grads):
        (mine_gu, mine_down), (far_gu, far_down) = grads
        gu = scatter_dp(mine_gu + other_y(far_gu))
        down = scatter_dp(mine_down + other_y(far_down))
        gu = seq_pieces(gu).reshape(4, rows, 2, dp_size, part)
        gu = gu.transpose(2, 1, 3, 0, 4).reshape(2, rows, ff).astype(jnp.float32)
        down = seq_pieces(down).reshape(4 * part, features).astype(jnp.float32)
        return gu[0], gu[1], down

    def reduce_out(grad):
        cut = grad.reshape(q_half, 2, out_half)
        kept = lax.dynamic_index_in_dim(cut, core, 1, keepdims=False)
        sent = lax.dynamic_index_in_dim(cut, 1 - core, 1, keepdims=False)
        cols = pair(core, kept, other_core(sent), axis=0)
        piece = scatter_dp(cols)
        summed = (piece.astype(jnp.float32) + other_y(piece).astype(jnp.float32)).astype(
            jnp.bfloat16
        )
        return pair(core, summed, other_core(summed), axis=1).astype(jnp.float32)

    def reduce_qkv(grad):
        piece = scatter_dp(grad)
        summed = (piece.astype(jnp.float32) + other_y(piece).astype(jnp.float32)).astype(
            jnp.bfloat16
        )
        got = other_core(summed)

        def joined(start, size):
            return pair(
                core, summed[:, start : start + size], got[:, start : start + size], axis=1
            ).astype(jnp.float32)

        return (
            joined(0, q_half),
            joined(q_half, k_half),
            joined(q_half + k_half, k_half),
            (summed[:, q_half + 2 * k_half :], got[:, q_half + 2 * k_half :]),
        )

    stream = regroup(tokens).astype(jnp.float32)
    all_weights = [gather_layer(layer) for layer in range(layers)]
    all_saved = []
    for layer in range(layers):
        stream, saved = forward(stream, all_weights[layer], gains[0, layer], gains[1, layer])
        all_saved.append(saved)
    output = ungroup(stream.astype(jnp.bfloat16))
    grad = regroup(cotangent).astype(jnp.float32)
    reduced = [None] * layers
    gain_grads = []
    for layer in reversed(range(layers)):
        grad, (mlp_g, out_g, qkv_g, one_g, two_g) = backward(
            grad, all_saved[layer], all_weights[layer], gains[0, layer], gains[1, layer]
        )
        gain_grads = [one_g, two_g] + gain_grads
        if layer == 0:
            extra = jnp.stack(gain_grads, axis=1)
            extra = jnp.pad(extra, ((0, 0), (0, 128 - extra.shape[1])))
            qkv_g = jnp.concatenate([qkv_g, extra.astype(jnp.bfloat16)], axis=1)
        reduced[layer] = (reduce_mlp(mlp_g), reduce_out(out_g), reduce_qkv(qkv_g))
    d_tokens = ungroup(grad)
    first, second = reduced[0][2][3]
    gain_out = first.astype(jnp.float32) + second.astype(jnp.float32)
    gain_out = gain_out[:, : 2 * layers].T.reshape(layers, 2, rows)

    def stacked(pick):
        return jnp.stack([pick(reduced[layer]) for layer in range(layers)])

    return (
        output,
        d_tokens,
        gain_out[:, 0],
        stacked(lambda r: r[2][0]),
        stacked(lambda r: r[2][1]),
        stacked(lambda r: r[2][2]),
        stacked(lambda r: r[1]),
        gain_out[:, 1],
        stacked(lambda r: r[0][0]),
        stacked(lambda r: r[0][1]),
        stacked(lambda r: r[0][2]),
    )


def solution(mesh):
    in_specs = (
        P("dp", "seq", None),
        P("dp", "seq", None),
        P(None, "dp"),
        P(None, "dp", None),
        P(None, "dp", None),
        P(None, "dp", None),
        P(None, "dp", None),
        P(None, "dp"),
        P(None, "dp", None),
        P(None, "dp", None),
        P(None, "dp", None),
    )
    return jax.shard_map(
        body, mesh=mesh, in_specs=in_specs, out_specs=in_specs, check_vma=False
    )
```

```python
import functools

import jax
import jax.numpy as jnp
from jax import lax
from jax.experimental import layout
from jax.experimental import pallas as pl
from jax.experimental.pallas import tpu as pltpu
from jax.sharding import PartitionSpec as P

HD = 96
SCALE = HD ** (-0.5)
EPSILON = 1e-05
ROPE_BASE = 100000.0

CORE_SWAP = [(0, 1), (1, 0), (2, 3), (3, 2)]
Y_SWAP = [(0, 2), (2, 0), (1, 3), (3, 1)]


BLOCKS = (0, 2, 1, 3)


def nt(left, right):
    return lax.dot_general(
        left, right, (((1,), (1,)), ((), ())), preferred_element_type=jnp.float32
    )


def nn(left, right):
    return lax.dot_general(
        left, right, (((1,), (0,)), ((), ())), preferred_element_type=jnp.float32
    )


def swap_halves(value):
    half = value.shape[1] // 2
    return jnp.concatenate([value[:, half:], value[:, :half]], axis=1)


def rope(value, cos, sin):
    return value * cos + swap_halves(value) * sin


def masked(scores, top):
    span = scores.shape[1] // 2
    key = lax.broadcasted_iota(jnp.int32, (span, 2 * span), 0)
    query = lax.broadcasted_iota(jnp.int32, (span, 2 * span), 1)
    query = jnp.where(query >= span, query - span, query)
    last = jnp.where(key <= query, scores[top:], -1e30)
    return last if top == 0 else jnp.concatenate([scores[:top], last], axis=0)


def masked_rows(scores, top):
    span = scores.shape[0] // 2
    key = lax.broadcasted_iota(jnp.int32, (2 * span, span), 1)
    query = lax.broadcasted_iota(jnp.int32, (2 * span, span), 0)
    query = jnp.where(query >= span, query - span, query)
    last = jnp.where(key <= query, scores[:, top:], -1e30)
    return last if top == 0 else jnp.concatenate([scores[:, :top], last], axis=1)


def forward_kernel(raw_ref, cos_ref, sin_ref, mixed_ref, q_ref, k_ref, v_ref, lse_ref, o_ref):
    heads = pl.program_id(0)
    span = raw_ref.shape[0] // 4
    count = mixed_ref.shape[1] // (2 * HD)
    for g in range(count):

        @pl.when(heads == g)
        def _(g=g):
            for part, block in enumerate(BLOCKS):
                here = pl.ds(part * span, span)
                there = pl.ds(block * span, span)
                cos, sin = cos_ref[here, :], sin_ref[here, :]
                for a in range(2):
                    at = (2 * g + a) * HD
                    q = rope(raw_ref[here, at : at + HD], cos, sin)
                    q_ref[0, pl.ds((2 * block + a) * span, span), :] = q.astype(jnp.bfloat16)
                at = (2 * count + g) * HD
                k_ref[0, there, :] = rope(raw_ref[here, at : at + HD], cos, sin).astype(
                    jnp.bfloat16
                )
                at = (3 * count + g) * HD
                v_ref[0, there, :] = raw_ref[here, at : at + HD].astype(jnp.bfloat16)

    for block in range(4):
        top, end = block * span, (block + 1) * span
        rows = pl.ds(2 * block * span, 2 * span)
        scores = masked_rows(nt(q_ref[0, rows, :], k_ref[0, :end, :]) * SCALE, top)
        highest = jnp.max(scores, axis=1, keepdims=True)
        powers = jnp.exp(scores - highest)
        total = jnp.sum(powers, axis=1, keepdims=True)
        probs = (powers * (1.0 / total)).astype(jnp.bfloat16)
        lse = jnp.broadcast_to(highest + jnp.log(total), (2 * span, 128))
        lse_ref[0, block : block + 1, :] = lse.T[:1]
        o_ref[rows, :] = nn(probs, v_ref[0, :end, :])
    for g in range(count):

        @pl.when(heads == g)
        def _(g=g):
            for part, block in enumerate(BLOCKS):
                here = pl.ds(part * span, span)
                both = [
                    o_ref[pl.ds((2 * block + a) * span, span), :].astype(jnp.bfloat16)
                    for a in range(2)
                ]
                mixed_ref[here, 2 * g * HD : (2 * g + 2) * HD] = jnp.concatenate(both, axis=1)


def attend_forward(raw, cos, sin):
    rows, width = raw.shape
    groups = width // (4 * HD)
    span = rows // 4
    whole = lambda shape: pl.BlockSpec(shape, lambda g: (0,) * len(shape))
    each = lambda shape: pl.BlockSpec((1,) + shape, lambda g: (g,) + (0,) * len(shape))
    return pl.pallas_call(
        forward_kernel,
        grid=(groups,),
        in_specs=[whole(raw.shape), whole(cos.shape), whole(sin.shape)],
        out_specs=[
            whole((rows, 2 * groups * HD)),
            each((2 * rows, HD)),
            each((rows, HD)),
            each((rows, HD)),
            each((4, 2 * span)),
        ],
        out_shape=[
            jax.ShapeDtypeStruct((rows, 2 * groups * HD), jnp.bfloat16),
            jax.ShapeDtypeStruct((groups, 2 * rows, HD), jnp.bfloat16),
            jax.ShapeDtypeStruct((groups, rows, HD), jnp.bfloat16),
            jax.ShapeDtypeStruct((groups, rows, HD), jnp.bfloat16),
            jax.ShapeDtypeStruct((groups, 4, 2 * span), jnp.float32),
        ],
        scratch_shapes=[pltpu.VMEM((2 * rows, HD), jnp.float32)],
        compiler_params=pltpu.CompilerParams(vmem_limit_bytes=48 * 1024 * 1024),
        cost_estimate=pl.CostEstimate(
            flops=20 * 10**9, bytes_accessed=15 * 10**6, transcendentals=6 * 10**6
        ),
        name="attention_forward",
    )(raw, cos, sin)


def backward_kernel(
    q_ref, k_ref, v_ref, lse_ref, grad_ref, cos_ref, sin_ref, out_ref, do_ref, dq_ref, dk_ref, dv_ref
):
    heads = pl.program_id(0)
    rows = k_ref.shape[1]
    span = rows // 4
    count = grad_ref.shape[1] // (2 * HD)
    for g in range(count):

        @pl.when(heads == g)
        def _(g=g):
            for part, block in enumerate(BLOCKS):
                here = pl.ds(part * span, span)
                for a in range(2):
                    at = (2 * g + a) * HD
                    do_ref[pl.ds((2 * block + a) * span, span), :] = grad_ref[
                        here, at : at + HD
                    ]

    key_t = k_ref[0].astype(jnp.float32).T.astype(jnp.bfloat16)
    for block in reversed(range(4)):
        top, end = block * span, (block + 1) * span
        at = pl.ds(2 * block * span, 2 * span)
        queries, grads = q_ref[0, at, :], do_ref[at, :]
        scores = masked(nt(k_ref[0, :end, :], queries) * SCALE, top)
        probs = jnp.exp(scores - lse_ref[0, block : block + 1, :])
        grad_probs = nt(v_ref[0, :end, :], grads)
        weighted = probs * grad_probs
        delta = jnp.sum(weighted, axis=0, keepdims=True)
        grad_scores = (probs * (grad_probs - delta)).astype(jnp.bfloat16)
        dv = nn(probs.astype(jnp.bfloat16), grads)
        dk = nn(grad_scores, queries)
        if block == 3:
            dv_ref[...] = dv
            dk_ref[...] = dk
        else:
            dv_ref[:end, :] += dv
            dk_ref[:end, :] += dk
        dq_ref[at, :] = nn(key_t[:, :end], grad_scores).T

    def low(value):
        return value.astype(jnp.bfloat16).astype(jnp.float32)

    for g in range(count):

        @pl.when(heads == g)
        def _(g=g):
            for part, block in enumerate(BLOCKS):
                here = pl.ds(part * span, span)
                there = pl.ds(block * span, span)
                cos, sin = cos_ref[here, :], -sin_ref[here, :]
                both = [
                    rope(low(dq_ref[pl.ds((2 * block + a) * span, span), :] * SCALE), cos, sin)
                    for a in range(2)
                ]
                out_ref[here, 2 * g * HD : (2 * g + 2) * HD] = jnp.concatenate(
                    both, axis=1
                ).astype(jnp.bfloat16)
                at = (2 * count + g) * HD
                out_ref[here, at : at + HD] = rope(
                    low(dk_ref[there, :] * SCALE), cos, sin
                ).astype(jnp.bfloat16)
                at = (3 * count + g) * HD
                out_ref[here, at : at + HD] = dv_ref[there, :].astype(jnp.bfloat16)


def attend_backward(q, k, v, lse, grad_mixed, cos, sin):
    groups, rows, _ = k.shape
    span = rows // 4
    whole = lambda shape: pl.BlockSpec(shape, lambda g: (0,) * len(shape))
    each = lambda shape: pl.BlockSpec((1,) + shape, lambda g: (g,) + (0,) * len(shape))
    return pl.pallas_call(
        backward_kernel,
        grid=(groups,),
        in_specs=[
            each((2 * rows, HD)),
            each((rows, HD)),
            each((rows, HD)),
            each((4, 2 * span)),
            whole(grad_mixed.shape),
            whole(cos.shape),
            whole(sin.shape),
        ],
        out_specs=whole((rows, 4 * groups * HD)),
        out_shape=jax.ShapeDtypeStruct((rows, 4 * groups * HD), jnp.bfloat16),
        scratch_shapes=[
            pltpu.VMEM((2 * rows, HD), jnp.bfloat16),
            pltpu.VMEM((2 * rows, HD), jnp.float32),
            pltpu.VMEM((rows, HD), jnp.float32),
            pltpu.VMEM((rows, HD), jnp.float32),
        ],
        compiler_params=pltpu.CompilerParams(vmem_limit_bytes=48 * 1024 * 1024),
        cost_estimate=pl.CostEstimate(
            flops=40 * 10**9, bytes_accessed=15 * 10**6, transcendentals=6 * 10**6
        ),
        name="attention_backward",
    )(q, k, v, lse, grad_mixed, cos, sin)


def other_core(value):
    return lax.ppermute(value, "seq", CORE_SWAP)


def other_y(value):
    return lax.ppermute(value, "seq", Y_SWAP)


def tie(value, *after):
    flat = value.reshape(-1, value.shape[-1])
    spec = pl.BlockSpec(memory_space=pltpu.HBM)
    tied = pl.pallas_call(
        lambda *refs: None,
        in_specs=[spec] * (1 + len(after)),
        out_specs=spec,
        out_shape=jax.ShapeDtypeStruct(flat.shape, flat.dtype),
        input_output_aliases={0: 0},
        name="tie",
    )(flat, *after)
    return tied.reshape(value.shape)


def gather_dp(piece):
    return lax.all_gather(piece, "dp", axis=0, tiled=True)


def dp_bits():
    count = lax.axis_size("dp").bit_length() - 1
    return [0] + list(range(count - 1, 0, -1))


def dp_swap(value, bit):
    size = lax.axis_size("dp")
    return lax.ppermute(value, "dp", [(d, d ^ (1 << bit)) for d in range(size)])


def by_bits(full):
    size = lax.axis_size("dp")
    count = size.bit_length() - 1
    return full.reshape((2,) * count + (full.shape[0] // size,) + full.shape[1:])


def halve(value, bit, left):
    axis = sorted(left, reverse=True).index(bit)
    own = (lax.axis_index("dp") >> bit) & 1
    kept = lax.dynamic_index_in_dim(value, own, axis, keepdims=False)
    sent = lax.dynamic_index_in_dim(value, 1 - own, axis, keepdims=False)
    return kept + dp_swap(sent, bit)


def halve_tied(value, bit, left, before):
    axis = sorted(left, reverse=True).index(bit)
    own = (lax.axis_index("dp") >> bit) & 1
    kept = lax.dynamic_index_in_dim(value, own, axis, keepdims=False)
    sent = lax.dynamic_index_in_dim(value, 1 - own, axis, keepdims=False)
    if before is not None:
        sent = tie(sent, before)
    got = dp_swap(sent, bit)
    return kept + got, got


def halve_all(value, order):
    for step, bit in enumerate(order):
        value = halve(value, bit, order[step:])
    return value


def scatter_dp(full):
    order = dp_bits()
    return halve_all(by_bits(full), order)


def double_dp(piece):
    order = dp_bits()[::-1]
    value = piece
    done = []
    for bit in order:
        got = dp_swap(value, bit)
        done.append(bit)
        axis = sorted(done, reverse=True).index(bit)
        own = (lax.axis_index("dp") >> bit) & 1
        value = pair(own, jnp.expand_dims(value, axis), jnp.expand_dims(got, axis), axis)
    return value.reshape((-1,) + piece.shape[1:])


def dot(left, right):
    return jnp.dot(left, right, preferred_element_type=jnp.float32)


def dot_t(left, right):
    return lax.dot_general(
        left, right, (((1,), (1,)), ((), ())), preferred_element_type=jnp.float32
    )


def tdot(left, right):
    out = lax.dot_general(
        left, right, (((0,), (0,)), ((), ())), preferred_element_type=jnp.float32
    ).astype(jnp.bfloat16)
    return layout.with_layout_constraint(out, layout.Layout(major_to_minor=(0, 1)))


def pair(flag, mine, other, axis=0):
    return jnp.where(
        flag == 0,
        jnp.concatenate([mine, other], axis=axis),
        jnp.concatenate([other, mine], axis=axis),
    )


def norm_rows(stream, gain):
    inverse = lax.rsqrt(jnp.mean(stream * stream, axis=-1, keepdims=True) + EPSILON)
    normed = stream * inverse
    return (normed, inverse, (normed * gain).astype(jnp.bfloat16))


def norm_back(grad_out, normed, inverse, gain):
    gain_grad = jnp.sum(grad_out * normed, axis=0)
    scaled = grad_out * gain
    grad_in = inverse * (scaled - normed * jnp.mean(scaled * normed, axis=-1, keepdims=True))
    return (grad_in, gain_grad)


def spread_kernel(part, *refs):
    ins, outs = refs[:-2], refs[-2:]
    layers = len(ins) // 2
    for layer in range(layers):

        @pl.when(pl.program_id(0) == layer)
        def _(pieces=(ins[layer], ins[layers + layer])):
            for piece, out in zip(pieces, outs):
                width = piece.shape[1] // 4
                for quarter in range(4):
                    for at in range(0, width, part):
                        to = 4 * at + quarter * part
                        start = quarter * width + at
                        out[0, :, to : to + part] = piece[:, start : start + part].astype(
                            jnp.float32
                        )


def spread_quarters(gates, ups, part):
    layers = len(gates)
    rows, width = gates[0].shape
    out = jax.ShapeDtypeStruct((layers, rows, width), jnp.float32)
    spec = pl.BlockSpec((1, rows, width), lambda layer: (layer, 0, 0))
    return pl.pallas_call(
        functools.partial(spread_kernel, part),
        grid=(layers,),
        in_specs=[pl.BlockSpec((rows, width), lambda layer: (0, 0))] * (2 * layers),
        out_specs=[spec, spec],
        out_shape=[out, out],
        compiler_params=pltpu.CompilerParams(vmem_limit_bytes=48 * 1024 * 1024),
        name="spread_quarters",
    )(*gates, *ups)


def body(
    tokens, cotangent, attn_norm, w_query, w_key, w_value, w_out, mlp_norm, w_gate, w_up, w_down
):
    dp_size = lax.axis_size("dp")
    index = lax.axis_index("seq")
    core = index % 2
    side = index // 2
    _, span, features = tokens.shape
    layers = w_query.shape[0]
    rows = w_query.shape[1]
    q_half = w_query.shape[2] // 2
    k_half = w_key.shape[2] // 2
    ff = w_gate.shape[2]
    part = ff // (4 * dp_size)
    ff_quarter = ff // 4
    out_half = features // 2
    heads = q_half // HD
    kv_heads = k_half // HD
    mine_rows = 2 * span
    length = 4 * span

    def regroup(*blocks):
        kept = [lax.dynamic_index_in_dim(block, side, 0, keepdims=False) for block in blocks]
        sent = [lax.dynamic_index_in_dim(block, 1 - side, 0, keepdims=False) for block in blocks]
        got = other_y(jnp.stack(sent))
        return [pair(side, mine, other) for mine, other in zip(kept, got)], got

    def ungroup(*blocks):
        halves = [block.reshape(2, span, features) for block in blocks]
        kept = [lax.dynamic_index_in_dim(half, side, 0, keepdims=False) for half in halves]
        sent = [lax.dynamic_index_in_dim(half, 1 - side, 0, keepdims=False) for half in halves]
        got = other_y(jnp.stack(sent).astype(jnp.bfloat16))
        return [
            pair(side, mine[None], other[None].astype(mine.dtype))
            for mine, other in zip(kept, got)
        ]

    def both_cores(value):
        return pair(core, value, other_core(value))

    def own_rows(total):
        kept = lax.dynamic_slice_in_dim(total, core * mine_rows, mine_rows, 0)
        sent = lax.dynamic_slice_in_dim(total, (1 - core) * mine_rows, mine_rows, 0)
        got = other_core(sent.astype(jnp.bfloat16))
        return kept + got.astype(jnp.float32)

    block_order = jnp.array([0, 2, 1, 3], jnp.int32)
    positions = (block_order[:, None] * span + jnp.arange(span)[None, :]).reshape(-1)
    middle = HD // 2
    frequency = ROPE_BASE ** (-jnp.arange(middle, dtype=jnp.float32) / middle)
    angles = positions.astype(jnp.float32)[:, None] * frequency[None, :]
    cosine = jnp.tile(jnp.cos(angles), (1, 2))
    sine = jnp.concatenate([-jnp.sin(angles), jnp.sin(angles)], axis=1)

    qkv_width = q_half + 2 * k_half
    gain_cols = jnp.pad(
        jnp.stack([attn_norm, mlp_norm]).reshape(2 * layers, rows).T,
        ((0, 0), (0, 128 - 2 * layers)),
    )

    def gather_layer(layer, before):
        local = [
            lax.dynamic_slice_in_dim(w_query[layer], core * q_half, q_half, 1),
            lax.dynamic_slice_in_dim(w_key[layer], core * k_half, k_half, 1),
            lax.dynamic_slice_in_dim(w_value[layer], core * k_half, k_half, 1),
            lax.dynamic_slice_in_dim(w_out[layer], core * out_half, out_half, 1),
        ]
        if layer == 0:
            local.append(gain_cols)

        def quarter(weight):
            cut = weight.reshape(rows, dp_size, 4, part)
            return lax.dynamic_index_in_dim(cut, index, 2, keepdims=False).reshape(rows, ff_quarter)

        local = jnp.concatenate(local, axis=1).reshape(2, rows // 2, -1)
        local = lax.dynamic_index_in_dim(local, side, 0, keepdims=False)
        near = gather_dp(local).reshape(dp_size, 1, rows // 2, -1)
        attention = pair(side, near, other_y(near), axis=1).reshape(features, -1)
        gate_up = jnp.concatenate([quarter(w_gate[layer]), quarter(w_up[layer])], axis=1)
        gate_up = gather_dp(gate_up if before is None else tie(gate_up, before))
        far_gate = other_y(gate_up[:, :ff_quarter])
        far_up = other_y(tie(gate_up[:, ff_quarter:], far_gate))
        qkv = attention[:, :qkv_width]
        out_cols = attention[:, qkv_width : qkv_width + out_half]
        kept = lax.dynamic_slice_in_dim(out_cols, core * q_half, q_half, 0)
        sent = lax.dynamic_slice_in_dim(out_cols, (1 - core) * q_half, q_half, 0)
        out = pair(core, kept, other_core(sent), axis=1)
        both = jnp.concatenate(
            [
                lax.dynamic_slice_in_dim(w_down[layer], index * part, part, 0),
                lax.dynamic_slice_in_dim(w_down[layer], (index ^ 2) * part, part, 0),
            ],
            axis=1,
        )
        both = gather_dp(both)
        down, far_down = both[:, :features], both[:, features:]
        weights = (qkv, out, (((gate_up,), down), ((far_gate, far_up), far_down)))
        return weights, attention[:, qkv_width + out_half :]

    def forward(stream, weights, gain_one, gain_two, ahead):
        qkv_w, out_w, mlp_w = weights
        normed_one, inverse_one, input_one = norm_rows(stream, gain_one)
        full_one = both_cores(input_one)
        if not ahead:
            full_one = tie(full_one, mlp_w[1][0][1])
        raw = dot(full_one, qkv_w)
        mixed, *attended = attend_forward(raw, cosine, sine)
        if ahead:
            mixed = tie(mixed, mlp_w[1][0][0])
        stream_two = stream + own_rows(dot(mixed, out_w))
        normed_two, inverse_two, input_two = norm_rows(stream_two, gain_two)
        full_two = both_cores(input_two)
        total = None
        kept_mlp = []
        for gate_up_w, down_w in mlp_w:
            if total is not None and ahead:
                full_two = tie(full_two, ahead[0])
            gate_up = [dot(full_two, weight) for weight in gate_up_w]
            if len(gate_up) == 1:
                gate_up = gate_up[0][:, :ff_quarter], gate_up[0][:, ff_quarter:]
            gate, up = gate_up
            hidden = (jax.nn.silu(gate) * up).astype(jnp.bfloat16)
            if total is not None and ahead:
                hidden = tie(hidden, ahead[1])
            term = dot(hidden, down_w)
            total = term if total is None else total + term
            kept_mlp.append((gate, up, hidden))
        result = stream_two + own_rows(total)
        saved = (
            normed_one,
            inverse_one,
            full_one,
            attended,
            mixed,
            normed_two,
            inverse_two,
            full_two,
            kept_mlp,
        )
        return result, saved

    def backward(grad, saved, weights, gain_one, gain_two):
        (
            normed_one,
            inverse_one,
            full_one,
            attended,
            mixed,
            normed_two,
            inverse_two,
            full_two,
            kept_mlp,
        ) = saved
        qkv_w, out_w, mlp_w = weights
        grad_full = both_cores(grad.astype(jnp.bfloat16))
        total = None
        down_grads = []
        gate_up_grads = []
        for (gate_up_w, down_w), (gate, up, hidden) in zip(mlp_w[::-1], kept_mlp[::-1]):
            down_grads.append(tdot(hidden, grad_full))
            grad_hidden = dot_t(grad_full, down_w)
            sig = jax.nn.sigmoid(gate)
            grad_gate = grad_hidden * up * sig * (1.0 + gate * (1.0 - sig))
            grad_up = grad_hidden * gate * sig
            grad_gate_up = jnp.concatenate([grad_gate, grad_up], axis=1).astype(jnp.bfloat16)
            gate_up_grads.append(tdot(full_two, grad_gate_up))
            if len(gate_up_w) == 1:
                terms = [dot_t(grad_gate_up, gate_up_w[0])]
            else:
                terms = [
                    dot_t(grad_gate_up[:, :ff_quarter], gate_up_w[0]),
                    dot_t(grad_gate_up[:, ff_quarter:], gate_up_w[1]),
                ]
            for term in terms:
                total = term if total is None else total + term
        mlp_grads = (gate_up_grads[::-1], down_grads[::-1])
        grad_two = own_rows(total)
        norm_two_in, gain_two_g = norm_back(grad_two, normed_two, inverse_two, gain_two)
        grad_mid = grad + norm_two_in
        mid_full = both_cores(grad_mid.astype(jnp.bfloat16))
        grad_out_w = tdot(mixed, mid_full)
        grad_mixed = dot_t(mid_full, out_w).astype(jnp.bfloat16)
        grad_qkv = attend_backward(*attended, grad_mixed, cosine, sine)
        grad_qkv_w = tdot(full_one, grad_qkv)
        grad_one = own_rows(dot_t(grad_qkv, qkv_w))
        norm_one_in, gain_one_g = norm_back(grad_one, normed_one, inverse_one, gain_one)
        points = (total, grad_qkv, grad_one, grad_full)
        parts = (mlp_grads, grad_out_w, grad_qkv_w, gain_one_g, gain_two_g)
        return grad_mid + norm_one_in, parts, points

    def finish(quarters, sums):
        joint = jnp.concatenate(quarters + sums, axis=1)
        got = other_y(joint)
        at = 0
        both = []
        for piece in quarters:
            width = piece.shape[1]
            both.append(pair(side, piece, got[:, at : at + width], axis=1))
            at += width
        if sums:
            added = joint[:, at:].astype(jnp.float32) + got[:, at:].astype(jnp.float32)
            both.append(added.astype(jnp.bfloat16))
        joint = jnp.concatenate(both, axis=1)
        got = other_core(joint)
        at = 0
        out = []
        for piece in quarters:
            width = 2 * piece.shape[1]
            cut = [v[:, at : at + width].reshape(-1, 2, 1, width // 2) for v in (joint, got)]
            out.append(pair(core, *cut, axis=2).reshape(-1, 2 * width))
            at += width
        for piece in sums:
            width = piece.shape[1]
            out.append(pair(core, joint[:, at : at + width], got[:, at : at + width], axis=1))
            at += width
        return out

    def finish_down(piece):
        (down,) = finish([piece], [])
        return (
            down.reshape(part, 4, features)
            .transpose(1, 0, 2)
            .reshape(4 * part, features)
            .astype(jnp.float32)
        )

    def cut_qkv(piece):
        halves = piece.reshape(piece.shape[0], 2, -1)
        at = 0
        cut = []
        for size in (q_half, k_half, k_half, halves.shape[2] - qkv_width):
            cut.append(halves[:, :, at : at + size].reshape(piece.shape[0], -1))
            at += size
        return cut

    def reduce_last(grads, out_grad, qkv_grad, points):
        after_mlp, after_attention, after_all, _ = points
        (mine_gu, far_gu), (mine_down, far_down) = grads
        order = dp_bits()

        def first(value, before):
            return halve_tied(by_bits(value), order[0], order, before)

        def rest(value, before):
            value, came = halve_tied(value, order[1], order[1:], before)
            for step in range(2, len(order)):
                value = halve(value, order[step], order[step:])
            return value, came

        got = other_y(far_down)
        down = mine_down + tie(got, after_mlp)
        got = other_y(tie(far_gu[:, :ff_quarter], got))
        gate = mine_gu[:, :ff_quarter] + tie(got, after_attention)
        got = other_y(tie(far_gu[:, ff_quarter:], got))
        up = mine_gu[:, ff_quarter:] + tie(got, after_all)
        down, came = first(down, None)
        out, came = first(out_grad, came)
        gate, came = first(gate, came)
        qkv, came = first(qkv_grad, came)
        up, came = first(up, came)
        down, came = rest(down, None)
        out, came = rest(out, came)
        gate, came = rest(gate, came)
        qkv, came = rest(qkv, came)
        up, came = rest(up, came)
        down = finish_down(down)
        gate, out, qkv = finish([gate], [out, qkv])
        (up,) = finish([up], [])
        return gate, up, down, out, cut_qkv(qkv)

    def reduce_first(grads, out_grad, qkv_grad, after):
        (mine_gu, far_gu), (mine_down, far_down) = grads
        width = mine_down.shape[1]
        piece = lax.psum_scatter(
            jnp.concatenate([mine_down, far_down], axis=1), "dp", scatter_dimension=0, tiled=True
        )
        down = piece[:, :width].astype(jnp.float32) + other_y(piece[:, width:]).astype(
            jnp.float32
        )
        gate_up = mine_gu + tie(other_y(far_gu), after)
        joint = jnp.concatenate([gate_up, out_grad, qkv_grad], axis=1)
        piece = lax.psum_scatter(joint, "dp", scatter_dimension=0, tiled=True)
        at = gate_up.shape[1]
        gate, up, out, qkv = finish(
            [piece[:, :ff_quarter], piece[:, ff_quarter:at]],
            [piece[:, at : at + out_half], piece[:, at + out_half :]],
        )
        return gate, up, finish_down(down.astype(jnp.bfloat16)), out, cut_qkv(qkv)

    def columns_of_core(grad):
        kept = lax.dynamic_slice_in_dim(grad, core * out_half, out_half, 1)
        sent = lax.dynamic_slice_in_dim(grad, (1 - core) * out_half, out_half, 1)
        return pair(core, kept, other_core(sent), axis=0)

    (stream, grad), came = regroup(tokens, cotangent)
    came = came.reshape(-1, features)
    gathered = [gather_layer(layer, came if layer == 0 else None) for layer in range(layers)]
    all_weights = [weights for weights, _ in gathered]
    gains = gathered[0][1][:, : 2 * layers].T.astype(jnp.float32)
    gains = gains.reshape(2, layers, features)
    stream, grad = stream.astype(jnp.float32), grad.astype(jnp.float32)
    all_saved = []
    for layer in range(layers):
        ahead = ()
        if layer + 1 < layers:
            near, far = all_weights[layer + 1][2]
            ahead = (near[0][0], far[0][0])
        stream, saved = forward(stream, all_weights[layer], gains[0, layer], gains[1, layer], ahead)
        all_saved.append(saved)
    reduced = [None] * layers
    gain_grads = []
    pending = []
    for layer in reversed(range(layers)):
        grad, (mlp_g, out_g, qkv_g, one_g, two_g), points = backward(
            grad, all_saved[layer], all_weights[layer], gains[0, layer], gains[1, layer]
        )
        gain_grads = [one_g, two_g] + gain_grads
        if layer == 0:
            extra = jnp.stack(gain_grads, axis=1)
            extra = jnp.pad(extra, ((0, 0), (0, 128 - extra.shape[1])))
            qkv_g = jnp.concatenate([qkv_g, extra.astype(jnp.bfloat16)], axis=1)
        pending.append((mlp_g, columns_of_core(out_g), qkv_g))
    *firsts, last = pending
    for layer, parts in zip(range(layers - 1, 0, -1), firsts):
        reduced[layer] = reduce_first(*parts, points[3])
    reduced[0] = reduce_last(*last, points)
    output, d_tokens = ungroup(stream, grad)
    output = output.astype(jnp.bfloat16)
    gain_out = reduced[0][4][3].reshape(rows, 2, -1)[:, :, : 2 * layers].astype(jnp.float32)
    gain_out = (gain_out[:, 0] + gain_out[:, 1]).T.reshape(layers, 2, rows)

    def stacked(pick):
        return jnp.stack([pick(reduced[layer]).astype(jnp.float32) for layer in range(layers)])

    return (
        output,
        d_tokens,
        gain_out[:, 0],
        stacked(lambda r: r[4][0]),
        stacked(lambda r: r[4][1]),
        stacked(lambda r: r[4][2]),
        stacked(lambda r: r[3]),
        gain_out[:, 1],
        *spread_quarters([r[0] for r in reduced], [r[1] for r in reduced], part),
        stacked(lambda r: r[2]),
    )


def solution(mesh):
    in_specs = (
        P("dp", "seq", None),
        P("dp", "seq", None),
        P(None, "dp"),
        P(None, "dp", None),
        P(None, "dp", None),
        P(None, "dp", None),
        P(None, "dp", None),
        P(None, "dp"),
        P(None, "dp", None),
        P(None, "dp", None),
        P(None, "dp", None),
    )
    return jax.shard_map(
        body, mesh=mesh, in_specs=in_specs, out_specs=in_specs, check_vma=False
    )
```

```python
import functools

import jax
import jax.numpy as jnp
from jax import lax
from jax.experimental import layout
from jax.experimental import pallas as pl
from jax.experimental.pallas import tpu as pltpu
from jax.sharding import PartitionSpec as P

HD = 96
SCALE = HD ** (-0.5)
EPSILON = 1e-05
ROPE_BASE = 100000.0

CORE_SWAP = [(0, 1), (1, 0), (2, 3), (3, 2)]
Y_SWAP = [(0, 2), (2, 0), (1, 3), (3, 1)]


BLOCKS = (0, 2, 1, 3)


SMALL = pl.CostEstimate(flops=10**6, bytes_accessed=10**6, transcendentals=0)


def nt(left, right):
    return lax.dot_general(
        left, right, (((1,), (1,)), ((), ())), preferred_element_type=jnp.float32
    )


def nn(left, right):
    return lax.dot_general(
        left, right, (((1,), (0,)), ((), ())), preferred_element_type=jnp.float32
    )


def swap_halves(value):
    half = value.shape[1] // 2
    return jnp.concatenate([value[:, half:], value[:, :half]], axis=1)


def rope(value, cos, sin):
    return value * cos + swap_halves(value) * sin


def masked(scores, top):
    span = scores.shape[1] // 2
    key = lax.broadcasted_iota(jnp.int32, (span, 2 * span), 0)
    query = lax.broadcasted_iota(jnp.int32, (span, 2 * span), 1)
    query = jnp.where(query >= span, query - span, query)
    last = jnp.where(key <= query, scores[top:], -1e30)
    return last if top == 0 else jnp.concatenate([scores[:top], last], axis=0)


def masked_rows(scores, top):
    span = scores.shape[0] // 2
    key = lax.broadcasted_iota(jnp.int32, (2 * span, span), 1)
    query = lax.broadcasted_iota(jnp.int32, (2 * span, span), 0)
    query = jnp.where(query >= span, query - span, query)
    last = jnp.where(key <= query, scores[:, top:], -1e30)
    return last if top == 0 else jnp.concatenate([scores[:, :top], last], axis=1)


def forward_kernel(raw_ref, cos_ref, sin_ref, mixed_ref, q_ref, k_ref, v_ref, lse_ref, o_ref):
    heads = pl.program_id(0)
    span = raw_ref.shape[0] // 4
    count = mixed_ref.shape[1] // (2 * HD)
    for g in range(count):

        @pl.when(heads == g)
        def _(g=g):
            for part, block in enumerate(BLOCKS):
                here = pl.ds(part * span, span)
                there = pl.ds(block * span, span)
                cos, sin = cos_ref[here, :], sin_ref[here, :]
                for a in range(2):
                    at = (2 * g + a) * HD
                    q = rope(raw_ref[here, at : at + HD], cos, sin)
                    q_ref[0, pl.ds((2 * block + a) * span, span), :] = q.astype(jnp.bfloat16)
                at = (2 * count + g) * HD
                k_ref[0, there, :] = rope(raw_ref[here, at : at + HD], cos, sin).astype(
                    jnp.bfloat16
                )
                at = (3 * count + g) * HD
                v_ref[0, there, :] = raw_ref[here, at : at + HD].astype(jnp.bfloat16)

    for block in range(4):
        top, end = block * span, (block + 1) * span
        rows = pl.ds(2 * block * span, 2 * span)
        scores = masked_rows(nt(q_ref[0, rows, :], k_ref[0, :end, :]) * SCALE, top)
        highest = jnp.max(scores, axis=1, keepdims=True)
        powers = jnp.exp(scores - highest)
        total = jnp.sum(powers, axis=1, keepdims=True)
        probs = (powers * (1.0 / total)).astype(jnp.bfloat16)
        lse = jnp.broadcast_to(highest + jnp.log(total), (2 * span, 128))
        lse_ref[0, block : block + 1, :] = lse.T[:1]
        o_ref[rows, :] = nn(probs, v_ref[0, :end, :])
    for g in range(count):

        @pl.when(heads == g)
        def _(g=g):
            for part, block in enumerate(BLOCKS):
                here = pl.ds(part * span, span)
                both = [
                    o_ref[pl.ds((2 * block + a) * span, span), :].astype(jnp.bfloat16)
                    for a in range(2)
                ]
                mixed_ref[here, 2 * g * HD : (2 * g + 2) * HD] = jnp.concatenate(both, axis=1)


def attend_forward(raw, cos, sin):
    rows, width = raw.shape
    groups = width // (4 * HD)
    span = rows // 4
    whole = lambda shape: pl.BlockSpec(shape, lambda g: (0,) * len(shape))
    each = lambda shape: pl.BlockSpec((1,) + shape, lambda g: (g,) + (0,) * len(shape))
    return pl.pallas_call(
        forward_kernel,
        grid=(groups,),
        in_specs=[whole(raw.shape), whole(cos.shape), whole(sin.shape)],
        out_specs=[
            whole((rows, 2 * groups * HD)),
            each((2 * rows, HD)),
            each((rows, HD)),
            each((rows, HD)),
            each((4, 2 * span)),
        ],
        out_shape=[
            jax.ShapeDtypeStruct((rows, 2 * groups * HD), jnp.bfloat16),
            jax.ShapeDtypeStruct((groups, 2 * rows, HD), jnp.bfloat16),
            jax.ShapeDtypeStruct((groups, rows, HD), jnp.bfloat16),
            jax.ShapeDtypeStruct((groups, rows, HD), jnp.bfloat16),
            jax.ShapeDtypeStruct((groups, 4, 2 * span), jnp.float32),
        ],
        scratch_shapes=[pltpu.VMEM((2 * rows, HD), jnp.float32)],
        compiler_params=pltpu.CompilerParams(vmem_limit_bytes=48 * 1024 * 1024),
        cost_estimate=SMALL,
        name="attention_forward",
    )(raw, cos, sin)


def backward_kernel(
    q_ref, k_ref, v_ref, lse_ref, grad_ref, cos_ref, sin_ref, out_ref, do_ref, dq_ref, dk_ref, dv_ref
):
    heads = pl.program_id(0)
    rows = k_ref.shape[1]
    span = rows // 4
    count = grad_ref.shape[1] // (2 * HD)
    for g in range(count):

        @pl.when(heads == g)
        def _(g=g):
            for part, block in enumerate(BLOCKS):
                here = pl.ds(part * span, span)
                for a in range(2):
                    at = (2 * g + a) * HD
                    do_ref[pl.ds((2 * block + a) * span, span), :] = grad_ref[
                        here, at : at + HD
                    ]

    key_t = k_ref[0].astype(jnp.float32).T.astype(jnp.bfloat16)
    for block in reversed(range(4)):
        top, end = block * span, (block + 1) * span
        at = pl.ds(2 * block * span, 2 * span)
        queries, grads = q_ref[0, at, :], do_ref[at, :]
        scores = masked(nt(k_ref[0, :end, :], queries) * SCALE, top)
        probs = jnp.exp(scores - lse_ref[0, block : block + 1, :])
        grad_probs = nt(v_ref[0, :end, :], grads)
        weighted = probs * grad_probs
        delta = jnp.sum(weighted, axis=0, keepdims=True)
        grad_scores = (probs * (grad_probs - delta)).astype(jnp.bfloat16)
        dv = nn(probs.astype(jnp.bfloat16), grads)
        dk = nn(grad_scores, queries)
        if block == 3:
            dv_ref[...] = dv
            dk_ref[...] = dk
        else:
            dv_ref[:end, :] += dv
            dk_ref[:end, :] += dk
        dq_ref[at, :] = nn(key_t[:, :end], grad_scores).T

    def low(value):
        return value.astype(jnp.bfloat16).astype(jnp.float32)

    for g in range(count):

        @pl.when(heads == g)
        def _(g=g):
            for part, block in enumerate(BLOCKS):
                here = pl.ds(part * span, span)
                there = pl.ds(block * span, span)
                cos, sin = cos_ref[here, :], -sin_ref[here, :]
                both = [
                    rope(low(dq_ref[pl.ds((2 * block + a) * span, span), :] * SCALE), cos, sin)
                    for a in range(2)
                ]
                out_ref[here, 2 * g * HD : (2 * g + 2) * HD] = jnp.concatenate(
                    both, axis=1
                ).astype(jnp.bfloat16)
                at = (2 * count + g) * HD
                out_ref[here, at : at + HD] = rope(
                    low(dk_ref[there, :] * SCALE), cos, sin
                ).astype(jnp.bfloat16)
                at = (3 * count + g) * HD
                out_ref[here, at : at + HD] = dv_ref[there, :].astype(jnp.bfloat16)


def attend_backward(q, k, v, lse, grad_mixed, cos, sin):
    groups, rows, _ = k.shape
    span = rows // 4
    whole = lambda shape: pl.BlockSpec(shape, lambda g: (0,) * len(shape))
    each = lambda shape: pl.BlockSpec((1,) + shape, lambda g: (g,) + (0,) * len(shape))
    return pl.pallas_call(
        backward_kernel,
        grid=(groups,),
        in_specs=[
            each((2 * rows, HD)),
            each((rows, HD)),
            each((rows, HD)),
            each((4, 2 * span)),
            whole(grad_mixed.shape),
            whole(cos.shape),
            whole(sin.shape),
        ],
        out_specs=whole((rows, 4 * groups * HD)),
        out_shape=jax.ShapeDtypeStruct((rows, 4 * groups * HD), jnp.bfloat16),
        scratch_shapes=[
            pltpu.VMEM((2 * rows, HD), jnp.bfloat16),
            pltpu.VMEM((2 * rows, HD), jnp.float32),
            pltpu.VMEM((rows, HD), jnp.float32),
            pltpu.VMEM((rows, HD), jnp.float32),
        ],
        compiler_params=pltpu.CompilerParams(vmem_limit_bytes=48 * 1024 * 1024),
        cost_estimate=SMALL,
        name="attention_backward",
    )(q, k, v, lse, grad_mixed, cos, sin)


def other_core(value):
    return lax.ppermute(value, "seq", CORE_SWAP)


def other_y(value):
    return lax.ppermute(value, "seq", Y_SWAP)


def tie(value, *after):
    flat = value.reshape(-1, value.shape[-1])
    spec = pl.BlockSpec(memory_space=pltpu.HBM)
    tied = pl.pallas_call(
        lambda *refs: None,
        in_specs=[spec] * (1 + len(after)),
        out_specs=spec,
        out_shape=jax.ShapeDtypeStruct(flat.shape, flat.dtype),
        input_output_aliases={0: 0},
        name="tie",
    )(flat, *after)
    return tied.reshape(value.shape)


def gather_dp(piece):
    return lax.all_gather(piece, "dp", axis=0, tiled=True)


def dp_bits():
    count = lax.axis_size("dp").bit_length() - 1
    return [0] + list(range(count - 1, 0, -1))


def dp_swap(value, bit):
    size = lax.axis_size("dp")
    return lax.ppermute(value, "dp", [(d, d ^ (1 << bit)) for d in range(size)])


def by_bits(full):
    size = lax.axis_size("dp")
    count = size.bit_length() - 1
    return full.reshape((2,) * count + (full.shape[0] // size,) + full.shape[1:])


def halve(value, bit, left):
    axis = sorted(left, reverse=True).index(bit)
    own = (lax.axis_index("dp") >> bit) & 1
    kept = lax.dynamic_index_in_dim(value, own, axis, keepdims=False)
    sent = lax.dynamic_index_in_dim(value, 1 - own, axis, keepdims=False)
    return kept + dp_swap(sent, bit)


def halve_tied(value, bit, left, before):
    axis = sorted(left, reverse=True).index(bit)
    own = (lax.axis_index("dp") >> bit) & 1
    kept = lax.dynamic_index_in_dim(value, own, axis, keepdims=False)
    sent = lax.dynamic_index_in_dim(value, 1 - own, axis, keepdims=False)
    if before is not None:
        sent = tie(sent, before)
    got = dp_swap(sent, bit)
    return kept + got, got


def halve_all(value, order):
    for step, bit in enumerate(order):
        value = halve(value, bit, order[step:])
    return value


def scatter_dp(full):
    order = dp_bits()
    return halve_all(by_bits(full), order)


def double_dp(piece):
    order = dp_bits()[::-1]
    value = piece
    done = []
    for bit in order:
        got = dp_swap(value, bit)
        done.append(bit)
        axis = sorted(done, reverse=True).index(bit)
        own = (lax.axis_index("dp") >> bit) & 1
        value = pair(own, jnp.expand_dims(value, axis), jnp.expand_dims(got, axis), axis)
    return value.reshape((-1,) + piece.shape[1:])


def dot(left, right):
    return jnp.dot(left, right, preferred_element_type=jnp.float32)


def dot_t(left, right):
    return lax.dot_general(
        left, right, (((1,), (1,)), ((), ())), preferred_element_type=jnp.float32
    )


def tdot(left, right):
    out = lax.dot_general(
        left, right, (((0,), (0,)), ((), ())), preferred_element_type=jnp.float32
    ).astype(jnp.bfloat16)
    return layout.with_layout_constraint(out, layout.Layout(major_to_minor=(0, 1)))


def pair(flag, mine, other, axis=0):
    return jnp.where(
        flag == 0,
        jnp.concatenate([mine, other], axis=axis),
        jnp.concatenate([other, mine], axis=axis),
    )


def norm_rows(stream, gain):
    inverse = lax.rsqrt(jnp.mean(stream * stream, axis=-1, keepdims=True) + EPSILON)
    normed = stream * inverse
    return (normed, inverse, (normed * gain).astype(jnp.bfloat16))


def norm_back(grad_out, normed, inverse, gain):
    gain_grad = jnp.sum(grad_out * normed, axis=0)
    scaled = grad_out * gain
    grad_in = inverse * (scaled - normed * jnp.mean(scaled * normed, axis=-1, keepdims=True))
    return (grad_in, gain_grad)


def mlp_back_kernel(*refs):
    grad_ref, input_t_ref, gate_ref, up_ref, gate_w_ref, up_w_ref, down_w_ref = refs[:7]
    before = refs[7:-4]
    total_ref, *out_refs = refs[-4:]
    step = pl.program_id(0)
    gate, up = gate_ref[...], up_ref[...]
    grad_hidden = nt(grad_ref[...], down_w_ref[...])
    sig = 1.0 / (1.0 + jnp.exp(-gate))
    swish = gate * sig
    grad_gate = (grad_hidden * up * (sig + swish * (1.0 - sig))).astype(jnp.bfloat16)
    grad_up = (grad_hidden * swish).astype(jnp.bfloat16)
    hidden_t = (swish * up).T.astype(jnp.bfloat16)
    term = nt(
        jnp.concatenate([grad_gate, grad_up], axis=1),
        jnp.concatenate([gate_w_ref[...], up_w_ref[...]], axis=1),
    )

    @pl.when(step == 0)
    def _():
        total_ref[...] = term

    @pl.when(step > 0)
    def _():
        total_ref[...] += term

    sums = [
        nn(input_t_ref[...], grad_gate),
        nn(input_t_ref[...], grad_up),
        nn(hidden_t, grad_ref[...]),
    ]
    for at, (out, value) in enumerate(zip(out_refs, sums)):
        if before:
            value = value + before[at][...].astype(jnp.float32)
        out[...] = value.astype(jnp.bfloat16)


def mlp_back(grad, input_t, gate_up, gate_up_w, down_w, before):
    tokens, features = grad.shape
    tile = 256
    width = down_w.shape[0]
    steps = width // tile

    def whole(shape):
        return pl.BlockSpec(shape, lambda t: (0, 0), pipeline_mode=pl.Buffered(1))

    def column(rows, first):
        return pl.BlockSpec((rows, tile), lambda t: (0, first + t))

    row = pl.BlockSpec((tile, features), lambda t: (t, 0))
    weight_specs = [column(features, 0), column(features, 0), row]
    return pl.pallas_call(
        mlp_back_kernel,
        grid=(steps,),
        in_specs=[
            whole(grad.shape),
            whole(input_t.shape),
            column(tokens, 0),
            column(tokens, steps),
            column(features, 0),
            column(features, steps),
            row,
            *(weight_specs if before else []),
        ],
        out_specs=[pl.BlockSpec((tokens, features), lambda t: (0, 0)), *weight_specs],
        out_shape=[
            jax.ShapeDtypeStruct((tokens, features), jnp.float32),
            jax.ShapeDtypeStruct((features, width), jnp.bfloat16),
            jax.ShapeDtypeStruct((features, width), jnp.bfloat16),
            jax.ShapeDtypeStruct((width, features), jnp.bfloat16),
        ],
        compiler_params=pltpu.CompilerParams(vmem_limit_bytes=60 * 1024 * 1024),
        cost_estimate=SMALL,
        name="mlp_backward",
    )(grad, input_t, gate_up, gate_up, gate_up_w, gate_up_w, down_w, *before)


def assemble_kernel(part, cuts, place_ref, *refs):
    groups = [refs[4 * i : 4 * i + 4] for i in range(len(cuts))]
    outs = refs[-cuts_outputs(cuts) :]
    for place in range(4):

        @pl.when(place_ref[0] == place)
        def _(place=place):
            for pieces, parts in zip(groups, cuts):
                by_place = {place ^ swap: ref for swap, ref in zip((0, 2, 1, 3), pieces)}
                for kind, at, size, out in parts:
                    here = slice(at, at + size)
                    if kind == "columns":
                        for quarter in range(4):
                            for start in range(0, size, part):
                                to = 4 * start + quarter * part
                                value = by_place[quarter][:, at + start : at + start + part]
                                outs[out][0, :, to : to + part] = value.astype(jnp.float32)
                    elif kind == "rows":
                        for quarter in range(4):
                            value = by_place[quarter][:, here].astype(jnp.float32)
                            outs[out][0, quarter * part : (quarter + 1) * part, :] = value
                    else:
                        halves = [
                            by_place[half][:, here].astype(jnp.float32)
                            + by_place[half + 2][:, here].astype(jnp.float32)
                            for half in range(2)
                        ]
                        if kind == "sum":
                            outs[out][0, :, :] = halves[0] + halves[1]
                        else:
                            for half in range(2):
                                outs[out][0, :, half * size : (half + 1) * size] = halves[half]


def cuts_outputs(cuts):
    return 1 + max(out for parts in cuts for *_, out in parts)


def assemble(place, layer, groups, cuts, shapes, part, before):
    operands = [piece for group in groups for piece in group]
    in_specs = [pl.BlockSpec(memory_space=pltpu.SMEM)]
    in_specs += [pl.BlockSpec(piece.shape, lambda i: (0, 0)) for piece in operands]
    aliases = {}
    if before is not None:
        aliases = {1 + len(operands) + i: i for i in range(len(before))}
        operands += before
        in_specs += [pl.BlockSpec(memory_space=pl.ANY)] * len(before)
    return pl.pallas_call(
        functools.partial(assemble_kernel, part, cuts),
        grid=(1,),
        in_specs=in_specs,
        out_specs=[pl.BlockSpec((1,) + shape[1:], lambda i: (layer, 0, 0)) for shape in shapes],
        out_shape=[jax.ShapeDtypeStruct(shape, jnp.float32) for shape in shapes],
        input_output_aliases=aliases,
        compiler_params=pltpu.CompilerParams(vmem_limit_bytes=60 * 1024 * 1024),
        name="assemble",
    )(place, *operands)


def body(
    tokens, cotangent, attn_norm, w_query, w_key, w_value, w_out, mlp_norm, w_gate, w_up, w_down
):
    dp_size = lax.axis_size("dp")
    index = lax.axis_index("seq")
    core = index % 2
    side = index // 2
    _, span, features = tokens.shape
    layers = w_query.shape[0]
    rows = w_query.shape[1]
    q_half = w_query.shape[2] // 2
    k_half = w_key.shape[2] // 2
    ff = w_gate.shape[2]
    part = ff // (4 * dp_size)
    ff_quarter = ff // 4
    out_half = features // 2
    heads = q_half // HD
    kv_heads = k_half // HD
    mine_rows = 2 * span
    length = 4 * span

    def regroup(*blocks):
        kept = [lax.dynamic_index_in_dim(block, side, 0, keepdims=False) for block in blocks]
        sent = [lax.dynamic_index_in_dim(block, 1 - side, 0, keepdims=False) for block in blocks]
        got = other_y(jnp.stack(sent))
        return [pair(side, mine, other) for mine, other in zip(kept, got)], got

    def swapped(block):
        halves = block.reshape(2, span, features)
        sent = lax.dynamic_index_in_dim(halves, 1 - side, 0, keepdims=False)
        return other_y(sent.astype(jnp.bfloat16))

    def ungroup(block, got):
        halves = block.reshape(2, span, features)
        kept = lax.dynamic_index_in_dim(halves, side, 0, keepdims=False)
        return pair(side, kept[None], got[None].astype(kept.dtype))

    def both_cores(value):
        return pair(core, value, other_core(value))

    def own_rows(total):
        kept = lax.dynamic_slice_in_dim(total, core * mine_rows, mine_rows, 0)
        sent = lax.dynamic_slice_in_dim(total, (1 - core) * mine_rows, mine_rows, 0)
        got = other_core(sent.astype(jnp.bfloat16))
        return kept + got.astype(jnp.float32)

    block_order = jnp.array([0, 2, 1, 3], jnp.int32)
    positions = (block_order[:, None] * span + jnp.arange(span)[None, :]).reshape(-1)
    middle = HD // 2
    frequency = ROPE_BASE ** (-jnp.arange(middle, dtype=jnp.float32) / middle)
    angles = positions.astype(jnp.float32)[:, None] * frequency[None, :]
    cosine = jnp.tile(jnp.cos(angles), (1, 2))
    sine = jnp.concatenate([-jnp.sin(angles), jnp.sin(angles)], axis=1)

    qkv_width = q_half + 2 * k_half
    gain_cols = jnp.pad(
        jnp.stack([attn_norm, mlp_norm]).reshape(2 * layers, rows).T,
        ((0, 0), (0, 128 - 2 * layers)),
    )

    (stream, grad), came = regroup(tokens, cotangent)
    came = came.reshape(-1, features)

    def attention_half(layer):
        local = [
            lax.dynamic_slice_in_dim(w_query[layer], core * q_half, q_half, 1),
            lax.dynamic_slice_in_dim(w_key[layer], core * k_half, k_half, 1),
            lax.dynamic_slice_in_dim(w_value[layer], core * k_half, k_half, 1),
            lax.dynamic_slice_in_dim(w_out[layer], core * out_half, out_half, 1),
        ]
        if layer == 0:
            local.append(gain_cols)
        local = jnp.concatenate(local, axis=1).reshape(2, rows // 2, -1)
        local = lax.dynamic_index_in_dim(local, side, 0, keepdims=False)
        return gather_dp(tie(local, came) if layer else local)

    def gather_layer(layer, near, far, before):
        def quarter(weight):
            cut = weight.reshape(rows, dp_size, 4, part)
            return lax.dynamic_index_in_dim(cut, index, 2, keepdims=False).reshape(rows, ff_quarter)

        near, far = (half.reshape(dp_size, 1, rows // 2, -1) for half in (near, far))
        attention = pair(side, near, far, axis=1).reshape(features, -1)
        gate_up = jnp.concatenate([quarter(w_gate[layer]), quarter(w_up[layer])], axis=1)
        gate_up = gather_dp(gate_up if before is None else tie(gate_up, before))
        qkv = attention[:, :qkv_width]
        out_cols = attention[:, qkv_width : qkv_width + out_half]
        kept = lax.dynamic_slice_in_dim(out_cols, core * q_half, q_half, 0)
        sent = lax.dynamic_slice_in_dim(out_cols, (1 - core) * q_half, q_half, 0)
        out = pair(core, kept, other_core(sent), axis=1)
        down = gather_dp(lax.dynamic_slice_in_dim(w_down[layer], index * part, part, 0))
        return (qkv, out, gate_up, down), attention[:, qkv_width + out_half :]

    def forward(stream, weights, gain_one, gain_two, ready):
        qkv_w, out_w, gate_up_w, down_w = weights
        normed_one, inverse_one, input_one = norm_rows(stream, gain_one)
        full_one = both_cores(input_one)
        raw = dot(full_one, qkv_w)
        mixed, *attended = attend_forward(raw, cosine, sine)
        mixed = tie(mixed, ready)
        stream_two = stream + own_rows(dot(mixed, out_w))
        normed_two, inverse_two, input_two = norm_rows(stream_two, gain_two)
        def turned(inputs):
            return layout.with_layout_constraint(
                inputs.T, layout.Layout(major_to_minor=(0, 1))
            )

        def hidden_of(gate_up):
            gate, up = gate_up[:, :ff_quarter], gate_up[:, ff_quarter:]
            return (jax.nn.silu(gate) * up).astype(jnp.bfloat16)

        far = other_y(input_two)
        near_in = both_cores(input_two)
        near_turned = turned(near_in)
        near_gate_up = dot(near_in, gate_up_w)
        near_total = dot(hidden_of(near_gate_up), down_w)
        far_in = both_cores(tie(far, near_gate_up, near_turned))
        far_gate_up = dot(far_in, gate_up_w)
        far_total = dot(hidden_of(far_gate_up), down_w)
        far_rows = own_rows(far_total).astype(jnp.bfloat16)
        far_turned = turned(far_in)
        far = tie(other_y(far_rows), far_turned)
        near = own_rows(tie(near_total, far_total))
        result = stream_two + (near + far.astype(jnp.float32))
        kept_mlp = [(near_turned, near_gate_up), (far_turned, far_gate_up)]
        saved = (
            normed_one,
            inverse_one,
            full_one,
            attended,
            mixed,
            normed_two,
            inverse_two,
            kept_mlp,
        )
        return result, saved

    def backward(grad, saved, weights, gain_one, gain_two, far, also):
        (
            normed_one,
            inverse_one,
            full_one,
            attended,
            mixed,
            normed_two,
            inverse_two,
            kept_mlp,
        ) = saved
        qkv_w, out_w, gate_up_w, down_w = weights
        grad_low = grad.astype(jnp.bfloat16)
        if far is None:
            far = other_y(grad_low)
        far, *mlp_grads = mlp_back(both_cores(far), *kept_mlp[1], gate_up_w, down_w, [])
        far_rows = own_rows(far).astype(jnp.bfloat16)
        far = other_y(far_rows)
        near = tie(both_cores(grad_low), far_rows)
        near, *mlp_grads = mlp_back(near, *kept_mlp[0], gate_up_w, down_w, mlp_grads)
        grad_two = own_rows(tie(near, far)) + far.astype(jnp.float32)
        norm_two_in, gain_two_g = norm_back(grad_two, normed_two, inverse_two, gain_two)
        grad_mid = grad + norm_two_in
        mid_full = both_cores(grad_mid.astype(jnp.bfloat16))
        grad_out_w = tdot(mixed, mid_full)
        grad_mixed = dot_t(mid_full, out_w).astype(jnp.bfloat16)
        grad_mixed = tie(grad_mixed, *also) if also else grad_mixed
        grad_qkv = attend_backward(*attended, grad_mixed, cosine, sine)
        grad_qkv_w = tdot(full_one, grad_qkv)
        grad_one = own_rows(dot_t(grad_qkv, qkv_w))
        norm_one_in, gain_one_g = norm_back(grad_one, normed_one, inverse_one, gain_one)
        grad = grad_mid + norm_one_in
        points = (mid_full, grad_qkv, grad_one)
        parts = (mlp_grads, grad_out_w, grad_qkv_w, gain_one_g, gain_two_g)
        return grad, parts, points

    def four(piece):
        got = other_y(piece)
        return [piece, got, other_core(piece), other_core(got)]

    def reduce_last(grads, out_grad, qkv_grad, points, earlier, grad):
        _, after_attention, after_all = points
        gate, up, down = grads
        order = dp_bits()
        last = {"x": None, "z": None, "any": after_attention}

        def send(value, step, link):
            value = by_bits(value) if step == 0 else value
            left = order[step:]
            axis = sorted(left, reverse=True).index(left[0])
            own = (lax.axis_index("dp") >> left[0]) & 1
            kept = lax.dynamic_index_in_dim(value, own, axis, keepdims=False)
            sent = lax.dynamic_index_in_dim(value, 1 - own, axis, keepdims=False)
            if link and last[link] is not None:
                sent = tie(sent, last[link])
            got = dp_swap(sent, left[0])
            if link:
                last[link] = got
            return kept, got

        def take(got):
            got = tie(got, last["any"])
            last["any"] = got
            return got

        def add(pending):
            return pending[0] + take(pending[1])

        def four_taken(piece):
            got = take(other_y(piece))
            return [piece, got, other_core(piece), other_core(got)]

        def finish(value):
            for step in range(2, len(order)):
                value = add(send(value, step, None))
            return value

        gate_up = send(jnp.concatenate([gate, up], axis=1), 0, "x")
        gate_up = send(add(gate_up), 1, "z")
        last["x"] = after_attention
        down = send(down, 0, "x")
        last["any"] = after_all
        out = send(out_grad, 0, "x")
        qkv = send(qkv_grad, 0, "x")
        down = send(add(down), 1, "z")
        out = send(add(out), 1, "z")
        earlier = [[four_taken(piece) for piece in pieces] for pieces in earlier]
        gate_up = finish(add(gate_up))
        qkv = send(add(qkv), 1, "z")
        grad = take(swapped(grad))
        gate_up = four_taken(gate_up)
        down = four_taken(finish(add(down)))
        out = finish(add(out))
        qkv = finish(add(qkv))
        joint = jnp.concatenate([out, qkv], axis=1)
        cuts = [
            [("columns", 0, ff_quarter, 0), ("columns", ff_quarter, ff_quarter, 1)],
            attention_cuts(0) + [("sum", joint.shape[1] - 128, 128, 7)],
            [("rows", 0, features, 2)],
        ]
        return ([gate_up, four(joint), down], cuts), earlier, grad

    def attention_cuts(at):
        sizes = (out_half, q_half, k_half, k_half)
        firsts = [at + sum(sizes[:i]) for i in range(4)]
        return [("halves", first, size, 3 + i) for i, (first, size) in enumerate(zip(firsts, sizes))]

    def reduce_first(grads, out_grad, qkv_grad, points):
        gate, up, down = grads
        down = lax.psum_scatter(down, "dp", scatter_dimension=0, tiled=True)
        joint = jnp.concatenate([gate, up, out_grad, qkv_grad], axis=1)
        piece = lax.psum_scatter(joint, "dp", scatter_dimension=0, tiled=True)
        cuts = [
            [("columns", 0, ff_quarter, 0), ("columns", ff_quarter, ff_quarter, 1)]
            + attention_cuts(2 * ff_quarter),
            [("rows", 0, features, 2)],
        ]
        return [piece, down], cuts

    def columns_of_core(grad):
        kept = lax.dynamic_slice_in_dim(grad, core * out_half, out_half, 1)
        sent = lax.dynamic_slice_in_dim(grad, (1 - core) * out_half, out_half, 1)
        return pair(core, kept, other_core(sent), axis=0)

    halves = [attention_half(layer) for layer in range(layers)]
    swapped_halves = []
    for half in halves:
        swapped_halves.append(other_y(tie(half, swapped_halves[-1]) if swapped_halves else half))
    swapped_halves[0] = tie(swapped_halves[0], *halves[1:])
    gathered = [
        gather_layer(layer, halves[layer], swapped_halves[layer], halves[1] if layer == 0 else None)
        for layer in range(layers)
    ]
    all_weights = [weights for weights, _ in gathered]
    gains = gathered[0][1][:, : 2 * layers].T.astype(jnp.float32)
    gains = gains.reshape(2, layers, features)
    stream, grad = stream.astype(jnp.float32), grad.astype(jnp.float32)
    far_cotangent = other_y(grad.astype(jnp.bfloat16))
    all_saved = []
    for layer in range(layers):
        ready = far_cotangent if layer == layers - 1 else swapped_halves[layer + 1]
        stream, saved = forward(
            stream, all_weights[layer], gains[0, layer], gains[1, layer], ready
        )
        all_saved.append(saved)
    also = [swapped(stream)]
    output = ungroup(stream, also[0]).astype(jnp.bfloat16)
    reduced = [None] * layers
    gain_grads = []
    for layer in reversed(range(layers)):
        grad, (mlp_g, out_g, qkv_g, one_g, two_g), points = backward(
            grad,
            all_saved[layer],
            all_weights[layer],
            gains[0, layer],
            gains[1, layer],
            far_cotangent if layer == layers - 1 else None,
            also,
        )
        gain_grads = [one_g, two_g] + gain_grads
        out_g = columns_of_core(out_g)
        if layer > 0:
            reduced[layer] = reduce_first(mlp_g, out_g, qkv_g, points)
            also = []
        else:
            extra = jnp.stack(gain_grads, axis=1)
            extra = jnp.pad(extra, ((0, 0), (0, 128 - extra.shape[1])))
            qkv_g = jnp.concatenate([qkv_g, extra.astype(jnp.bfloat16)], axis=1)
            earlier = [reduced[at][0] for at in range(1, layers)]
            reduced[0], earlier, got = reduce_last(mlp_g, out_g, qkv_g, points, earlier, grad)
    d_tokens = ungroup(grad, got)
    for layer in range(1, layers):
        reduced[layer] = earlier[layer - 1], reduced[layer][1]
    shapes = [(layers, rows, ff)] * 2 + [(layers, 4 * part, features)]
    shapes += [(layers, rows, 2 * size) for size in (out_half, q_half, k_half, k_half)]
    place = index.astype(jnp.int32).reshape(1)
    outs = None
    for layer in range(layers - 1, 0, -1):
        outs = assemble(place, layer, *reduced[layer], shapes, part, outs)
    outs = assemble(place, 0, *reduced[0], shapes + [(1, rows, 128)], part, outs)
    gate_out, up_out, down_out, out_out, query_out, key_out, value_out, gain_out = outs
    gain_out = gain_out[0, :, : 2 * layers].T.reshape(layers, 2, rows)
    return (
        output,
        d_tokens,
        gain_out[:, 0],
        query_out,
        key_out,
        value_out,
        out_out,
        gain_out[:, 1],
        gate_out,
        up_out,
        down_out,
    )


def solution(mesh):
    in_specs = (
        P("dp", "seq", None),
        P("dp", "seq", None),
        P(None, "dp"),
        P(None, "dp", None),
        P(None, "dp", None),
        P(None, "dp", None),
        P(None, "dp", None),
        P(None, "dp"),
        P(None, "dp", None),
        P(None, "dp", None),
        P(None, "dp", None),
    )
    return jax.shard_map(
        body, mesh=mesh, in_specs=in_specs, out_specs=in_specs, check_vma=False
    )
```

```python
import functools

import jax
import jax.numpy as jnp
from jax import lax
from jax.experimental import layout
from jax.experimental import pallas as pl
from jax.experimental.pallas import tpu as pltpu
from jax.sharding import PartitionSpec as P

HD = 96
SCALE = HD ** (-0.5)
EPSILON = 1e-05
ROPE_BASE = 100000.0

CORE_SWAP = [(0, 1), (1, 0), (2, 3), (3, 2)]
Y_SWAP = [(0, 2), (2, 0), (1, 3), (3, 1)]


BLOCKS = (0, 2, 1, 3)


SMALL = pl.CostEstimate(flops=10**6, bytes_accessed=10**6, transcendentals=0)


def nt(left, right):
    return lax.dot_general(
        left, right, (((1,), (1,)), ((), ())), preferred_element_type=jnp.float32
    )


def nn(left, right):
    return lax.dot_general(
        left, right, (((1,), (0,)), ((), ())), preferred_element_type=jnp.float32
    )


def swap_halves(value):
    half = value.shape[1] // 2
    return jnp.concatenate([value[:, half:], value[:, :half]], axis=1)


def rope(value, cos, sin):
    return value * cos + swap_halves(value) * sin


def masked(scores, top):
    span = scores.shape[1] // 2
    key = lax.broadcasted_iota(jnp.int32, (span, 2 * span), 0)
    query = lax.broadcasted_iota(jnp.int32, (span, 2 * span), 1)
    query = jnp.where(query >= span, query - span, query)
    last = jnp.where(key <= query, scores[top:], -1e30)
    return last if top == 0 else jnp.concatenate([scores[:top], last], axis=0)


def masked_rows(scores, top):
    span = scores.shape[0] // 2
    key = lax.broadcasted_iota(jnp.int32, (2 * span, span), 1)
    query = lax.broadcasted_iota(jnp.int32, (2 * span, span), 0)
    query = jnp.where(query >= span, query - span, query)
    last = jnp.where(key <= query, scores[:, top:], -1e30)
    return last if top == 0 else jnp.concatenate([scores[:, :top], last], axis=1)


def forward_kernel(raw_ref, cos_ref, sin_ref, mixed_ref, q_ref, k_ref, v_ref, lse_ref, o_ref):
    heads = pl.program_id(0)
    span = raw_ref.shape[0] // 4
    count = mixed_ref.shape[1] // (2 * HD)
    for g in range(count):

        @pl.when(heads == g)
        def _(g=g):
            for part, block in enumerate(BLOCKS):
                here = pl.ds(part * span, span)
                there = pl.ds(block * span, span)
                cos, sin = cos_ref[here, :], sin_ref[here, :]
                for a in range(2):
                    at = (2 * g + a) * HD
                    q = rope(raw_ref[here, at : at + HD], cos, sin)
                    q_ref[0, pl.ds((2 * block + a) * span, span), :] = q.astype(jnp.bfloat16)
                at = (2 * count + g) * HD
                k_ref[0, there, :] = rope(raw_ref[here, at : at + HD], cos, sin).astype(
                    jnp.bfloat16
                )
                at = (3 * count + g) * HD
                v_ref[0, there, :] = raw_ref[here, at : at + HD].astype(jnp.bfloat16)

    for block in range(4):
        top, end = block * span, (block + 1) * span
        rows = pl.ds(2 * block * span, 2 * span)
        scores = masked_rows(nt(q_ref[0, rows, :], k_ref[0, :end, :]) * SCALE, top)
        highest = jnp.max(scores, axis=1, keepdims=True)
        powers = jnp.exp(scores - highest)
        total = jnp.sum(powers, axis=1, keepdims=True)
        probs = (powers * (1.0 / total)).astype(jnp.bfloat16)
        lse = jnp.broadcast_to(highest + jnp.log(total), (2 * span, 128))
        lse_ref[0, block : block + 1, :] = lse.T[:1]
        o_ref[rows, :] = nn(probs, v_ref[0, :end, :])
    for g in range(count):

        @pl.when(heads == g)
        def _(g=g):
            for part, block in enumerate(BLOCKS):
                here = pl.ds(part * span, span)
                both = [
                    o_ref[pl.ds((2 * block + a) * span, span), :].astype(jnp.bfloat16)
                    for a in range(2)
                ]
                mixed_ref[here, 2 * g * HD : (2 * g + 2) * HD] = jnp.concatenate(both, axis=1)


def attend_forward(raw, cos, sin):
    rows, width = raw.shape
    groups = width // (4 * HD)
    span = rows // 4
    whole = lambda shape: pl.BlockSpec(shape, lambda g: (0,) * len(shape))
    each = lambda shape: pl.BlockSpec((1,) + shape, lambda g: (g,) + (0,) * len(shape))
    return pl.pallas_call(
        forward_kernel,
        grid=(groups,),
        in_specs=[whole(raw.shape), whole(cos.shape), whole(sin.shape)],
        out_specs=[
            whole((rows, 2 * groups * HD)),
            each((2 * rows, HD)),
            each((rows, HD)),
            each((rows, HD)),
            each((4, 2 * span)),
        ],
        out_shape=[
            jax.ShapeDtypeStruct((rows, 2 * groups * HD), jnp.bfloat16),
            jax.ShapeDtypeStruct((groups, 2 * rows, HD), jnp.bfloat16),
            jax.ShapeDtypeStruct((groups, rows, HD), jnp.bfloat16),
            jax.ShapeDtypeStruct((groups, rows, HD), jnp.bfloat16),
            jax.ShapeDtypeStruct((groups, 4, 2 * span), jnp.float32),
        ],
        scratch_shapes=[pltpu.VMEM((2 * rows, HD), jnp.float32)],
        compiler_params=pltpu.CompilerParams(vmem_limit_bytes=48 * 1024 * 1024),
        cost_estimate=SMALL,
        name="attention_forward",
    )(raw, cos, sin)


def backward_kernel(
    q_ref, k_ref, v_ref, lse_ref, grad_ref, cos_ref, sin_ref, out_ref, do_ref, dq_ref, dk_ref, dv_ref
):
    heads = pl.program_id(0)
    rows = k_ref.shape[1]
    span = rows // 4
    count = grad_ref.shape[1] // (2 * HD)
    for g in range(count):

        @pl.when(heads == g)
        def _(g=g):
            for part, block in enumerate(BLOCKS):
                here = pl.ds(part * span, span)
                for a in range(2):
                    at = (2 * g + a) * HD
                    do_ref[pl.ds((2 * block + a) * span, span), :] = grad_ref[
                        here, at : at + HD
                    ]

    key_t = k_ref[0].astype(jnp.float32).T.astype(jnp.bfloat16)
    for block in reversed(range(4)):
        top, end = block * span, (block + 1) * span
        at = pl.ds(2 * block * span, 2 * span)
        queries, grads = q_ref[0, at, :], do_ref[at, :]
        scores = masked(nt(k_ref[0, :end, :], queries) * SCALE, top)
        probs = jnp.exp(scores - lse_ref[0, block : block + 1, :])
        grad_probs = nt(v_ref[0, :end, :], grads)
        weighted = probs * grad_probs
        delta = jnp.sum(weighted, axis=0, keepdims=True)
        grad_scores = (probs * (grad_probs - delta)).astype(jnp.bfloat16)
        dv = nn(probs.astype(jnp.bfloat16), grads)
        dk = nn(grad_scores, queries)
        if block == 3:
            dv_ref[...] = dv
            dk_ref[...] = dk
        else:
            dv_ref[:end, :] += dv
            dk_ref[:end, :] += dk
        dq_ref[at, :] = nn(key_t[:, :end], grad_scores).T

    def low(value):
        return value.astype(jnp.bfloat16).astype(jnp.float32)

    for g in range(count):

        @pl.when(heads == g)
        def _(g=g):
            for part, block in enumerate(BLOCKS):
                here = pl.ds(part * span, span)
                there = pl.ds(block * span, span)
                cos, sin = cos_ref[here, :], -sin_ref[here, :]
                both = [
                    rope(low(dq_ref[pl.ds((2 * block + a) * span, span), :] * SCALE), cos, sin)
                    for a in range(2)
                ]
                out_ref[here, 2 * g * HD : (2 * g + 2) * HD] = jnp.concatenate(
                    both, axis=1
                ).astype(jnp.bfloat16)
                at = (2 * count + g) * HD
                out_ref[here, at : at + HD] = rope(
                    low(dk_ref[there, :] * SCALE), cos, sin
                ).astype(jnp.bfloat16)
                at = (3 * count + g) * HD
                out_ref[here, at : at + HD] = dv_ref[there, :].astype(jnp.bfloat16)


def attend_backward(q, k, v, lse, grad_mixed, cos, sin):
    groups, rows, _ = k.shape
    span = rows // 4
    whole = lambda shape: pl.BlockSpec(shape, lambda g: (0,) * len(shape))
    each = lambda shape: pl.BlockSpec((1,) + shape, lambda g: (g,) + (0,) * len(shape))
    return pl.pallas_call(
        backward_kernel,
        grid=(groups,),
        in_specs=[
            each((2 * rows, HD)),
            each((rows, HD)),
            each((rows, HD)),
            each((4, 2 * span)),
            whole(grad_mixed.shape),
            whole(cos.shape),
            whole(sin.shape),
        ],
        out_specs=whole((rows, 4 * groups * HD)),
        out_shape=jax.ShapeDtypeStruct((rows, 4 * groups * HD), jnp.bfloat16),
        scratch_shapes=[
            pltpu.VMEM((2 * rows, HD), jnp.bfloat16),
            pltpu.VMEM((2 * rows, HD), jnp.float32),
            pltpu.VMEM((rows, HD), jnp.float32),
            pltpu.VMEM((rows, HD), jnp.float32),
        ],
        compiler_params=pltpu.CompilerParams(vmem_limit_bytes=48 * 1024 * 1024),
        cost_estimate=SMALL,
        name="attention_backward",
    )(q, k, v, lse, grad_mixed, cos, sin)


def other_core(value):
    return lax.ppermute(value, "seq", CORE_SWAP)


def other_y(value):
    return lax.ppermute(value, "seq", Y_SWAP)


def tie(value, *after):
    flat = value.reshape(-1, value.shape[-1])
    spec = pl.BlockSpec(memory_space=pltpu.HBM)
    tied = pl.pallas_call(
        lambda *refs: None,
        in_specs=[spec] * (1 + len(after)),
        out_specs=spec,
        out_shape=jax.ShapeDtypeStruct(flat.shape, flat.dtype),
        input_output_aliases={0: 0},
        name="tie",
    )(flat, *after)
    return tied.reshape(value.shape)


def gather_dp(piece):
    return lax.all_gather(piece, "dp", axis=0, tiled=True)


def dp_bits():
    count = lax.axis_size("dp").bit_length() - 1
    return [0] + list(range(count - 1, 0, -1))


def dp_swap(value, bit):
    size = lax.axis_size("dp")
    return lax.ppermute(value, "dp", [(d, d ^ (1 << bit)) for d in range(size)])


def by_bits(full):
    size = lax.axis_size("dp")
    count = size.bit_length() - 1
    return full.reshape((2,) * count + (full.shape[0] // size,) + full.shape[1:])


def halve(value, bit, left):
    axis = sorted(left, reverse=True).index(bit)
    own = (lax.axis_index("dp") >> bit) & 1
    kept = lax.dynamic_index_in_dim(value, own, axis, keepdims=False)
    sent = lax.dynamic_index_in_dim(value, 1 - own, axis, keepdims=False)
    return kept + dp_swap(sent, bit)


def halve_tied(value, bit, left, before):
    axis = sorted(left, reverse=True).index(bit)
    own = (lax.axis_index("dp") >> bit) & 1
    kept = lax.dynamic_index_in_dim(value, own, axis, keepdims=False)
    sent = lax.dynamic_index_in_dim(value, 1 - own, axis, keepdims=False)
    if before is not None:
        sent = tie(sent, before)
    got = dp_swap(sent, bit)
    return kept + got, got


def halve_all(value, order):
    for step, bit in enumerate(order):
        value = halve(value, bit, order[step:])
    return value


def scatter_dp(full):
    order = dp_bits()
    return halve_all(by_bits(full), order)


def double_dp(piece):
    order = dp_bits()[::-1]
    value = piece
    done = []
    for bit in order:
        got = dp_swap(value, bit)
        done.append(bit)
        axis = sorted(done, reverse=True).index(bit)
        own = (lax.axis_index("dp") >> bit) & 1
        value = pair(own, jnp.expand_dims(value, axis), jnp.expand_dims(got, axis), axis)
    return value.reshape((-1,) + piece.shape[1:])


def dot(left, right):
    return jnp.dot(left, right, preferred_element_type=jnp.float32)


def dot_t(left, right):
    return lax.dot_general(
        left, right, (((1,), (1,)), ((), ())), preferred_element_type=jnp.float32
    )


def tdot(left, right):
    out = lax.dot_general(
        left, right, (((0,), (0,)), ((), ())), preferred_element_type=jnp.float32
    ).astype(jnp.bfloat16)
    return layout.with_layout_constraint(out, layout.Layout(major_to_minor=(0, 1)))


def pair(flag, mine, other, axis=0):
    return jnp.where(
        flag == 0,
        jnp.concatenate([mine, other], axis=axis),
        jnp.concatenate([other, mine], axis=axis),
    )


def norm_rows(stream, gain):
    inverse = lax.rsqrt(jnp.mean(stream * stream, axis=-1, keepdims=True) + EPSILON)
    normed = stream * inverse
    return (normed, inverse, (normed * gain).astype(jnp.bfloat16))


def norm_back(grad_out, normed, inverse, gain):
    gain_grad = jnp.sum(grad_out * normed, axis=0)
    scaled = grad_out * gain
    grad_in = inverse * (scaled - normed * jnp.mean(scaled * normed, axis=-1, keepdims=True))
    return (grad_in, gain_grad)


def mlp_back_kernel(*refs):
    grad_ref, input_t_ref, gate_ref, up_ref, gate_w_ref, up_w_ref, down_w_ref = refs[:7]
    before = refs[7:-4]
    total_ref, *out_refs = refs[-4:]
    step = pl.program_id(0)
    pieces = []
    size = gate_ref.shape[0] // 4
    for piece in range(4):
        rows = pl.ds(piece * size, size)
        gate, up = gate_ref[rows, :], up_ref[rows, :]
        grad_hidden = nt(grad_ref[rows, :], down_w_ref[...])
        sig = 1.0 / (1.0 + jnp.exp(-gate))
        swish = gate * sig
        grad_gate = grad_hidden * up * (sig + swish * (1.0 - sig))
        pieces.append(
            (
                grad_gate.astype(jnp.bfloat16),
                (grad_hidden * swish).astype(jnp.bfloat16),
                (swish * up).T.astype(jnp.bfloat16),
            )
        )
    grad_gate, grad_up, hidden_t = (
        jnp.concatenate(part, axis=axis) for part, axis in zip(zip(*pieces), (0, 0, 1))
    )
    term = nt(
        jnp.concatenate([grad_gate, grad_up], axis=1),
        jnp.concatenate([gate_w_ref[...], up_w_ref[...]], axis=1),
    )

    @pl.when(step == 0)
    def _():
        total_ref[...] = term

    @pl.when(step > 0)
    def _():
        total_ref[...] += term

    sums = [
        nn(input_t_ref[...], grad_gate),
        nn(input_t_ref[...], grad_up),
        nn(hidden_t, grad_ref[...]),
    ]
    for at, (out, value) in enumerate(zip(out_refs, sums)):
        if before:
            value = value + before[at][...].astype(jnp.float32)
        out[...] = value.astype(jnp.bfloat16)


def mlp_back(grad, input_t, gate_up, gate_up_w, down_w, before):
    tokens, features = grad.shape
    tile = 256
    width = down_w.shape[0]
    steps = width // tile

    def whole(shape):
        return pl.BlockSpec(shape, lambda t: (0, 0), pipeline_mode=pl.Buffered(1))

    def column(rows, first):
        return pl.BlockSpec((rows, tile), lambda t: (0, first + t))

    row = pl.BlockSpec((tile, features), lambda t: (t, 0))
    weight_specs = [column(features, 0), column(features, 0), row]
    return pl.pallas_call(
        mlp_back_kernel,
        grid=(steps,),
        in_specs=[
            whole(grad.shape),
            whole(input_t.shape),
            column(tokens, 0),
            column(tokens, steps),
            column(features, 0),
            column(features, steps),
            row,
            *(weight_specs if before else []),
        ],
        out_specs=[pl.BlockSpec((tokens, features), lambda t: (0, 0)), *weight_specs],
        out_shape=[
            jax.ShapeDtypeStruct((tokens, features), jnp.float32),
            jax.ShapeDtypeStruct((features, width), jnp.bfloat16),
            jax.ShapeDtypeStruct((features, width), jnp.bfloat16),
            jax.ShapeDtypeStruct((width, features), jnp.bfloat16),
        ],
        compiler_params=pltpu.CompilerParams(vmem_limit_bytes=60 * 1024 * 1024),
        cost_estimate=SMALL,
        name="mlp_backward",
    )(grad, input_t, gate_up, gate_up, gate_up_w, gate_up_w, down_w, *before)


def assemble_kernel(part, cuts, place_ref, *refs):
    groups = [refs[4 * i : 4 * i + 4] for i in range(len(cuts))]
    outs = refs[-cuts_outputs(cuts) :]
    for place in range(4):

        @pl.when(place_ref[0] == place)
        def _(place=place):
            for pieces, parts in zip(groups, cuts):
                by_place = {place ^ swap: ref for swap, ref in zip((0, 2, 1, 3), pieces)}
                for kind, at, size, out in parts:
                    here = slice(at, at + size)
                    if kind == "columns":
                        for quarter in range(4):
                            for start in range(0, size, part):
                                to = 4 * start + quarter * part
                                value = by_place[quarter][:, at + start : at + start + part]
                                outs[out][0, :, to : to + part] = value.astype(jnp.float32)
                    elif kind == "rows":
                        for quarter in range(4):
                            value = by_place[quarter][:, here].astype(jnp.float32)
                            outs[out][0, quarter * part : (quarter + 1) * part, :] = value
                    elif kind in ("blocks", "gains"):
                        for half in range(2):
                            values = [by_place[2 * half + core][:, here] for core in range(2)]
                            values = [value.astype(jnp.float32) for value in values]
                            count = values[0].shape[0]
                            to = slice(half * count, (half + 1) * count)
                            if kind == "gains":
                                outs[out][0, to, :] = values[0] + values[1]
                            else:
                                outs[out][0, to, :size] = values[0]
                                outs[out][0, to, size:] = values[1]
                    else:
                        halves = [
                            by_place[half][:, here].astype(jnp.float32)
                            + by_place[half + 2][:, here].astype(jnp.float32)
                            for half in range(2)
                        ]
                        for half in range(2):
                            outs[out][0, :, half * size : (half + 1) * size] = halves[half]


def cuts_outputs(cuts):
    return 1 + max(out for parts in cuts for *_, out in parts)


def assemble(place, layer, groups, cuts, shapes, part, before):
    operands = [piece for group in groups for piece in group]
    in_specs = [pl.BlockSpec(memory_space=pltpu.SMEM)]
    in_specs += [pl.BlockSpec(piece.shape, lambda i: (0, 0)) for piece in operands]
    aliases = {}
    if before is not None:
        aliases = {1 + len(operands) + i: i for i in range(len(before))}
        operands += before
        in_specs += [pl.BlockSpec(memory_space=pl.ANY)] * len(before)
    return pl.pallas_call(
        functools.partial(assemble_kernel, part, cuts),
        grid=(1,),
        in_specs=in_specs,
        out_specs=[pl.BlockSpec((1,) + shape[1:], lambda i: (layer, 0, 0)) for shape in shapes],
        out_shape=[jax.ShapeDtypeStruct(shape, jnp.float32) for shape in shapes],
        input_output_aliases=aliases,
        compiler_params=pltpu.CompilerParams(vmem_limit_bytes=60 * 1024 * 1024),
        name="assemble",
    )(place, *operands)


def body(
    tokens, cotangent, attn_norm, w_query, w_key, w_value, w_out, mlp_norm, w_gate, w_up, w_down
):
    dp_size = lax.axis_size("dp")
    index = lax.axis_index("seq")
    core = index % 2
    side = index // 2
    _, span, features = tokens.shape
    layers = w_query.shape[0]
    rows = w_query.shape[1]
    q_half = w_query.shape[2] // 2
    k_half = w_key.shape[2] // 2
    ff = w_gate.shape[2]
    part = ff // (4 * dp_size)
    ff_quarter = ff // 4
    out_half = features // 2
    heads = q_half // HD
    kv_heads = k_half // HD
    mine_rows = 2 * span
    length = 4 * span

    def regroup(*blocks):
        kept = [lax.dynamic_index_in_dim(block, side, 0, keepdims=False) for block in blocks]
        sent = [lax.dynamic_index_in_dim(block, 1 - side, 0, keepdims=False) for block in blocks]
        got = other_y(jnp.stack(sent))
        return [pair(side, mine, other) for mine, other in zip(kept, got)], got

    def swapped(block):
        halves = block.reshape(2, span, features)
        sent = lax.dynamic_index_in_dim(halves, 1 - side, 0, keepdims=False)
        return other_y(sent.astype(jnp.bfloat16))

    def ungroup(block, got):
        halves = block.reshape(2, span, features)
        kept = lax.dynamic_index_in_dim(halves, side, 0, keepdims=False)
        return pair(side, kept[None], got[None].astype(kept.dtype))

    def both_cores(value):
        return pair(core, value, other_core(value))

    def own_rows(total):
        kept = lax.dynamic_slice_in_dim(total, core * mine_rows, mine_rows, 0)
        sent = lax.dynamic_slice_in_dim(total, (1 - core) * mine_rows, mine_rows, 0)
        got = other_core(sent.astype(jnp.bfloat16))
        return kept + got.astype(jnp.float32)

    block_order = jnp.array([0, 2, 1, 3], jnp.int32)
    positions = (block_order[:, None] * span + jnp.arange(span)[None, :]).reshape(-1)
    middle = HD // 2
    frequency = ROPE_BASE ** (-jnp.arange(middle, dtype=jnp.float32) / middle)
    angles = positions.astype(jnp.float32)[:, None] * frequency[None, :]
    cosine = jnp.tile(jnp.cos(angles), (1, 2))
    sine = jnp.concatenate([-jnp.sin(angles), jnp.sin(angles)], axis=1)

    qkv_width = q_half + 2 * k_half
    gain_cols = jnp.pad(
        jnp.stack([attn_norm, mlp_norm]).reshape(2 * layers, rows).T,
        ((0, 0), (0, 128 - 2 * layers)),
    )

    (stream, grad), came = regroup(tokens, cotangent)
    came = came.reshape(-1, features)

    def quarter(weight):
        cut = weight.reshape(rows, dp_size, 4, part)
        return lax.dynamic_index_in_dim(cut, index, 2, keepdims=False).reshape(rows, ff_quarter)

    def attention_local(layer):
        local = [
            lax.dynamic_slice_in_dim(w_query[layer], core * q_half, q_half, 1),
            lax.dynamic_slice_in_dim(w_key[layer], core * k_half, k_half, 1),
            lax.dynamic_slice_in_dim(w_value[layer], core * k_half, k_half, 1),
            lax.dynamic_slice_in_dim(w_out[layer], core * out_half, out_half, 1),
        ]
        if layer == 0:
            local.insert(3, gain_cols)
        local = jnp.concatenate(local, axis=1).reshape(2, rows // 2, -1)
        return lax.dynamic_index_in_dim(local, side, 0, keepdims=False)

    gate_up_locals = [
        jnp.concatenate([quarter(w_gate[layer]), quarter(w_up[layer])], axis=1)
        for layer in range(layers)
    ]
    down_locals = [
        lax.dynamic_slice_in_dim(w_down[layer], index * part, part, 0) for layer in range(layers)
    ]
    halves = [gather_dp(attention_local(0))]
    for layer in range(1, layers):
        halves.append(gather_dp(tie(attention_local(layer), came, *gate_up_locals, *down_locals)))

    def joined(near, far):
        near, far = (half.reshape(dp_size, 1, rows // 2, -1) for half in (near, far))
        return pair(side, near, far, axis=1).reshape(features, -1)

    firsts = halves[0].shape[1] - out_half
    far_qkv = other_y(halves[0][:, :firsts])
    far_out = other_y(tie(halves[0][:, firsts:], far_qkv))
    last_far = far_out
    fars = []
    for layer in range(1, layers):
        last_far = other_y(tie(halves[layer], last_far))
        fars.append(last_far)
    far_qkv = tie(far_qkv, *halves[1:])
    first_qkv = joined(halves[0][:, :firsts], far_qkv)
    attention_weights = [(first_qkv[:, :qkv_width], joined(halves[0][:, firsts:], far_out))]
    for near, far in zip(halves[1:], fars):
        joint = joined(near, far)
        attention_weights.append((joint[:, :qkv_width], joint[:, qkv_width:]))
    all_weights = []
    for layer in range(layers):
        gate_up = gate_up_locals[layer]
        gate_up = gather_dp(tie(gate_up, halves[1]) if layer == 0 else gate_up)
        down = gather_dp(down_locals[layer])
        qkv, out_cols = attention_weights[layer]
        kept = lax.dynamic_slice_in_dim(out_cols, core * q_half, q_half, 0)
        sent = lax.dynamic_slice_in_dim(out_cols, (1 - core) * q_half, q_half, 0)
        out = pair(core, kept, other_core(sent), axis=1)
        all_weights.append((qkv, out, gate_up, down))
    gains = first_qkv[:, qkv_width : qkv_width + 2 * layers].T.astype(jnp.float32)
    gains = gains.reshape(2, layers, features)

    def forward(stream, weights, gain_one, gain_two, ready, last):
        qkv_w, out_w, gate_up_w, down_w = weights
        normed_one, inverse_one, input_one = norm_rows(stream, gain_one)
        full_one = both_cores(input_one)
        raw = dot(full_one, qkv_w)
        mixed, *attended = attend_forward(raw, cosine, sine)
        mixed = tie(mixed, ready)
        stream_two = stream + own_rows(dot(mixed, out_w))
        normed_two, inverse_two, input_two = norm_rows(stream_two, gain_two)
        def turned(inputs):
            return layout.with_layout_constraint(
                inputs.T, layout.Layout(major_to_minor=(0, 1))
            )

        def hidden_of(gate_up):
            gate, up = gate_up[:, :ff_quarter], gate_up[:, ff_quarter:]
            return (jax.nn.silu(gate) * up).astype(jnp.bfloat16)

        far = other_y(input_two)
        near_in = both_cores(input_two)
        near_turned = turned(near_in)
        near_gate_up = dot(near_in, gate_up_w)
        far_in = both_cores(tie(far, near_gate_up, near_turned))
        far_gate_up = dot(far_in, gate_up_w)
        far_turned = turned(far_in)

        def down_dots(after):
            pieces = [near_gate_up, far_gate_up]
            if after is not None:
                pieces = [tie(piece, after) for piece in pieces]
            return [dot(hidden_of(piece), down_w) for piece in pieces]

        def finish(totals, meanwhile):
            near_total, far_total = totals
            far_rows = own_rows(far_total).astype(jnp.bfloat16)
            far = tie(other_y(far_rows), meanwhile)
            near = own_rows(tie(near_total, far_total))
            return stream_two + (near + far.astype(jnp.float32))

        result = (down_dots, finish) if last else finish(down_dots(None), far_turned)
        kept_mlp = [(near_turned, near_gate_up), (far_turned, far_gate_up)]
        saved = (
            normed_one,
            inverse_one,
            full_one,
            attended,
            mixed,
            normed_two,
            inverse_two,
            kept_mlp,
        )
        return result, saved

    def backward(grad, saved, weights, gain_one, gain_two, far, fill):
        (
            normed_one,
            inverse_one,
            full_one,
            attended,
            mixed,
            normed_two,
            inverse_two,
            kept_mlp,
        ) = saved
        qkv_w, out_w, gate_up_w, down_w = weights
        grad_low = grad.astype(jnp.bfloat16)
        late = None
        if fill is not None:
            down_dots, finish = fill
            totals = down_dots(grad_low)
            far = tie(other_y(grad_low), *totals)
        far, *mlp_grads = mlp_back(both_cores(far), *kept_mlp[1], gate_up_w, down_w, [])
        far_rows = own_rows(far).astype(jnp.bfloat16)
        far = other_y(far_rows)
        if fill is not None:
            late = finish(totals, far)
        near = tie(both_cores(grad_low), far_rows)
        near, *mlp_grads = mlp_back(near, *kept_mlp[0], gate_up_w, down_w, mlp_grads)
        grad_two = own_rows(tie(near, far)) + far.astype(jnp.float32)
        norm_two_in, gain_two_g = norm_back(grad_two, normed_two, inverse_two, gain_two)
        grad_mid = grad + norm_two_in
        mid_full = both_cores(grad_mid.astype(jnp.bfloat16))
        grad_out_w = tdot(mixed, mid_full)
        grad_mixed = dot_t(mid_full, out_w).astype(jnp.bfloat16)
        if late is not None:
            got = swapped(late)
            grad_mixed = tie(grad_mixed, got, grad_out_w)
            late = (late, got)
        grad_qkv = attend_backward(*attended, grad_mixed, cosine, sine)
        grad_qkv_w = tdot(full_one, grad_qkv)
        low = grad_qkv if fill is None else tie(grad_qkv, grad_qkv_w)
        grad_one = own_rows(dot_t(low, qkv_w))
        norm_one_in, gain_one_g = norm_back(grad_one, normed_one, inverse_one, gain_one)
        grad = grad_mid + norm_one_in
        points = (mid_full, grad_qkv, grad_one)
        parts = (mlp_grads, grad_out_w, grad_qkv_w, gain_one_g, gain_two_g)
        return grad, parts, points, late

    def four(piece):
        got = other_y(piece)
        return [piece, got, other_core(piece), other_core(got)]

    def reduce_last(grads, out_grad, qkv_grad, points, earlier, grad):
        _, after_attention, after_all = points
        gate, up, down = grads
        order = dp_bits()
        last = {"x": None, "z": None, "any": after_attention}

        def send(value, step, link):
            value = by_bits(value) if step == 0 else value
            left = order[step:]
            axis = sorted(left, reverse=True).index(left[0])
            own = (lax.axis_index("dp") >> left[0]) & 1
            kept = lax.dynamic_index_in_dim(value, own, axis, keepdims=False)
            sent = lax.dynamic_index_in_dim(value, 1 - own, axis, keepdims=False)
            if link and last[link] is not None:
                sent = tie(sent, last[link])
            got = dp_swap(sent, left[0])
            if link:
                last[link] = got
            return kept, got

        def take(got):
            got = tie(got, last["any"])
            last["any"] = got
            return got

        def add(pending):
            return pending[0] + take(pending[1])

        def four_taken(piece):
            got = take(other_y(piece))
            return [piece, got, other_core(piece), other_core(got)]

        def finish(value):
            for step in range(2, len(order)):
                value = add(send(value, step, None))
            return value

        def sides(value):
            cut = value.reshape(dp_size, 2, rows // 2, -1)
            kept = lax.dynamic_index_in_dim(cut, side, 1, keepdims=False)
            sent = lax.dynamic_index_in_dim(cut, 1 - side, 1, keepdims=False)
            shape = (features // 2, -1)
            return kept.reshape(shape), sent.reshape(shape)

        gate_up = send(jnp.concatenate([gate, up], axis=1), 0, "x")
        out_near, sent = sides(out_grad)
        out_far = other_y(sent)
        qkv_near, sent = sides(qkv_grad)
        qkv_far = other_y(tie(sent, out_far))
        gate_up = send(add(gate_up), 1, "z")
        last["x"] = tie(after_attention, last["x"].reshape(-1, last["x"].shape[-1]))
        down = send(down, 0, "x")
        down = send(add(down), 1, "z")
        out = send(out_near + take(out_far), 0, "x")
        out = send(add(out), 1, "z")
        gate_up = finish(add(gate_up))
        qkv = send(qkv_near + take(qkv_far), 0, "x")
        down = finish(add(down))
        earlier = [[four_taken(piece) for piece in pieces] for pieces in earlier]
        out = finish(add(out))
        qkv = send(add(qkv), 1, "z")
        gate_up = four_taken(gate_up)
        down = four_taken(down)
        got_grad = take(swapped(grad))
        qkv = finish(add(qkv))
        joint = jnp.concatenate([out, qkv], axis=1)
        cuts = [
            [("columns", 0, ff_quarter, 0), ("columns", ff_quarter, ff_quarter, 1)],
            attention_cuts(0, "blocks") + [("gains", joint.shape[1] - 128, 128, 7)],
            [("rows", 0, features, 2)],
        ]
        return ([gate_up, four(joint), down], cuts), earlier, got_grad

    def attention_cuts(at, kind="halves"):
        sizes = (out_half, q_half, k_half, k_half)
        firsts = [at + sum(sizes[:i]) for i in range(4)]
        return [(kind, first, size, 3 + i) for i, (first, size) in enumerate(zip(firsts, sizes))]

    def reduce_first(grads, out_grad, qkv_grad, points):
        gate, up, down = grads
        down = lax.psum_scatter(down, "dp", scatter_dimension=0, tiled=True)
        joint = jnp.concatenate([gate, up, out_grad, qkv_grad], axis=1)
        piece = lax.psum_scatter(joint, "dp", scatter_dimension=0, tiled=True)
        cuts = [
            [("columns", 0, ff_quarter, 0), ("columns", ff_quarter, ff_quarter, 1)]
            + attention_cuts(2 * ff_quarter),
            [("rows", 0, features, 2)],
        ]
        return [piece, down], cuts

    def columns_of_core(grad):
        kept = lax.dynamic_slice_in_dim(grad, core * out_half, out_half, 1)
        sent = lax.dynamic_slice_in_dim(grad, (1 - core) * out_half, out_half, 1)
        return pair(core, kept, other_core(sent), axis=0)

    stream, grad = stream.astype(jnp.float32), grad.astype(jnp.float32)
    far_cotangent = other_y(grad.astype(jnp.bfloat16))
    all_saved = []
    for layer in range(layers):
        ready = far_cotangent if layer == layers - 1 else fars[layer]
        stream, saved = forward(
            stream, all_weights[layer], gains[0, layer], gains[1, layer], ready, layer == layers - 1
        )
        all_saved.append(saved)
    reduced = [None] * layers
    gain_grads = []
    for layer in reversed(range(layers)):
        grad, (mlp_g, out_g, qkv_g, one_g, two_g), points, late = backward(
            grad,
            all_saved[layer],
            all_weights[layer],
            gains[0, layer],
            gains[1, layer],
            far_cotangent if layer == layers - 1 else None,
            stream if layer == 0 else None,
        )
        gain_grads = [one_g, two_g] + gain_grads
        out_g = columns_of_core(out_g)
        if layer > 0:
            reduced[layer] = reduce_first(mlp_g, out_g, qkv_g, points)
        else:
            extra = jnp.stack(gain_grads, axis=1)
            extra = jnp.pad(extra, ((0, 0), (0, 128 - extra.shape[1])))
            qkv_g = jnp.concatenate([qkv_g, extra.astype(jnp.bfloat16)], axis=1)
            earlier = [reduced[at][0] for at in range(1, layers)]
            reduced[0], earlier, got = reduce_last(
                mlp_g, out_g, qkv_g, points, earlier, grad
            )
    output = ungroup(*late).astype(jnp.bfloat16)
    d_tokens = ungroup(grad, got)
    for layer in range(1, layers):
        reduced[layer] = earlier[layer - 1], reduced[layer][1]
    shapes = [(layers, rows, ff)] * 2 + [(layers, 4 * part, features)]
    shapes += [(layers, rows, 2 * size) for size in (out_half, q_half, k_half, k_half)]
    place = index.astype(jnp.int32).reshape(1)
    outs = None
    for layer in range(layers - 1, 0, -1):
        outs = assemble(place, layer, *reduced[layer], shapes, part, outs)
    outs = assemble(place, 0, *reduced[0], shapes + [(1, rows, 128)], part, outs)
    gate_out, up_out, down_out, out_out, query_out, key_out, value_out, gain_out = outs
    gain_out = gain_out[0, :, : 2 * layers].T.reshape(layers, 2, rows)
    return (
        output,
        d_tokens,
        gain_out[:, 0],
        query_out,
        key_out,
        value_out,
        out_out,
        gain_out[:, 1],
        gate_out,
        up_out,
        down_out,
    )


def solution(mesh):
    in_specs = (
        P("dp", "seq", None),
        P("dp", "seq", None),
        P(None, "dp"),
        P(None, "dp", None),
        P(None, "dp", None),
        P(None, "dp", None),
        P(None, "dp", None),
        P(None, "dp"),
        P(None, "dp", None),
        P(None, "dp", None),
        P(None, "dp", None),
    )
    return jax.shard_map(
        body, mesh=mesh, in_specs=in_specs, out_specs=in_specs, check_vma=False
    )
```

```python
import functools

import jax
import jax.numpy as jnp
from jax import lax
from jax.experimental import layout
from jax.experimental import pallas as pl
from jax.experimental.pallas import tpu as pltpu
from jax.sharding import PartitionSpec as P

HD = 96
SCALE = HD ** (-0.5)
EPSILON = 1e-05
ROPE_BASE = 100000.0

CORE_SWAP = [(0, 1), (1, 0), (2, 3), (3, 2)]
Y_SWAP = [(0, 2), (2, 0), (1, 3), (3, 1)]


BLOCKS = (0, 2, 1, 3)


SMALL = pl.CostEstimate(flops=10**6, bytes_accessed=10**6, transcendentals=0)


def nt(left, right):
    return lax.dot_general(
        left, right, (((1,), (1,)), ((), ())), preferred_element_type=jnp.float32
    )


def nn(left, right):
    return lax.dot_general(
        left, right, (((1,), (0,)), ((), ())), preferred_element_type=jnp.float32
    )


def swap_halves(value):
    half = value.shape[1] // 2
    return jnp.concatenate([value[:, half:], value[:, :half]], axis=1)


def rope(value, cos, sin):
    return value * cos + swap_halves(value) * sin


def masked(scores, top):
    span = scores.shape[1] // 2
    key = lax.broadcasted_iota(jnp.int32, (span, 2 * span), 0)
    query = lax.broadcasted_iota(jnp.int32, (span, 2 * span), 1)
    query = jnp.where(query >= span, query - span, query)
    last = jnp.where(key <= query, scores[top:], -1e30)
    return last if top == 0 else jnp.concatenate([scores[:top], last], axis=0)


def masked_rows(scores, top):
    span = scores.shape[0] // 2
    key = lax.broadcasted_iota(jnp.int32, (2 * span, span), 1)
    query = lax.broadcasted_iota(jnp.int32, (2 * span, span), 0)
    query = jnp.where(query >= span, query - span, query)
    last = jnp.where(key <= query, scores[:, top:], -1e30)
    return last if top == 0 else jnp.concatenate([scores[:, :top], last], axis=1)


def forward_kernel(raw_ref, cos_ref, sin_ref, mixed_ref, q_ref, k_ref, v_ref, lse_ref, o_ref):
    heads = pl.program_id(0)
    span = raw_ref.shape[0] // 4
    count = mixed_ref.shape[1] // (2 * HD)
    for g in range(count):

        @pl.when(heads == g)
        def _(g=g):
            for part, block in enumerate(BLOCKS):
                here = pl.ds(part * span, span)
                there = pl.ds(block * span, span)
                cos, sin = cos_ref[here, :], sin_ref[here, :]
                for a in range(2):
                    at = (2 * g + a) * HD
                    q = rope(raw_ref[here, at : at + HD], cos, sin)
                    q_ref[0, pl.ds((2 * block + a) * span, span), :] = q.astype(jnp.bfloat16)
                at = (2 * count + g) * HD
                k_ref[0, there, :] = rope(raw_ref[here, at : at + HD], cos, sin).astype(
                    jnp.bfloat16
                )
                at = (3 * count + g) * HD
                v_ref[0, there, :] = raw_ref[here, at : at + HD].astype(jnp.bfloat16)

    for block in range(4):
        top, end = block * span, (block + 1) * span
        rows = pl.ds(2 * block * span, 2 * span)
        scores = masked_rows(nt(q_ref[0, rows, :], k_ref[0, :end, :]) * SCALE, top)
        highest = jnp.max(scores, axis=1, keepdims=True)
        powers = jnp.exp(scores - highest)
        total = jnp.sum(powers, axis=1, keepdims=True)
        probs = (powers * (1.0 / total)).astype(jnp.bfloat16)
        lse = jnp.broadcast_to(highest + jnp.log(total), (2 * span, 128))
        lse_ref[0, block : block + 1, :] = lse.T[:1]
        o_ref[rows, :] = nn(probs, v_ref[0, :end, :])
    for g in range(count):

        @pl.when(heads == g)
        def _(g=g):
            for part, block in enumerate(BLOCKS):
                here = pl.ds(part * span, span)
                both = [
                    o_ref[pl.ds((2 * block + a) * span, span), :].astype(jnp.bfloat16)
                    for a in range(2)
                ]
                mixed_ref[here, 2 * g * HD : (2 * g + 2) * HD] = jnp.concatenate(both, axis=1)


def attend_forward(raw, cos, sin):
    rows, width = raw.shape
    groups = width // (4 * HD)
    span = rows // 4
    whole = lambda shape: pl.BlockSpec(shape, lambda g: (0,) * len(shape))
    each = lambda shape: pl.BlockSpec((1,) + shape, lambda g: (g,) + (0,) * len(shape))
    return pl.pallas_call(
        forward_kernel,
        grid=(groups,),
        in_specs=[whole(raw.shape), whole(cos.shape), whole(sin.shape)],
        out_specs=[
            whole((rows, 2 * groups * HD)),
            each((2 * rows, HD)),
            each((rows, HD)),
            each((rows, HD)),
            each((4, 2 * span)),
        ],
        out_shape=[
            jax.ShapeDtypeStruct((rows, 2 * groups * HD), jnp.bfloat16),
            jax.ShapeDtypeStruct((groups, 2 * rows, HD), jnp.bfloat16),
            jax.ShapeDtypeStruct((groups, rows, HD), jnp.bfloat16),
            jax.ShapeDtypeStruct((groups, rows, HD), jnp.bfloat16),
            jax.ShapeDtypeStruct((groups, 4, 2 * span), jnp.float32),
        ],
        scratch_shapes=[pltpu.VMEM((2 * rows, HD), jnp.float32)],
        compiler_params=pltpu.CompilerParams(vmem_limit_bytes=48 * 1024 * 1024),
        cost_estimate=SMALL,
        name="attention_forward",
    )(raw, cos, sin)


def backward_kernel(
    q_ref, k_ref, v_ref, lse_ref, grad_ref, cos_ref, sin_ref, out_ref, do_ref, dq_ref, dk_ref, dv_ref
):
    heads = pl.program_id(0)
    rows = k_ref.shape[1]
    span = rows // 4
    count = grad_ref.shape[1] // (2 * HD)
    for g in range(count):

        @pl.when(heads == g)
        def _(g=g):
            for part, block in enumerate(BLOCKS):
                here = pl.ds(part * span, span)
                for a in range(2):
                    at = (2 * g + a) * HD
                    do_ref[pl.ds((2 * block + a) * span, span), :] = grad_ref[
                        here, at : at + HD
                    ]

    key_t = k_ref[0].astype(jnp.float32).T.astype(jnp.bfloat16)
    for block in reversed(range(4)):
        top, end = block * span, (block + 1) * span
        at = pl.ds(2 * block * span, 2 * span)
        queries, grads = q_ref[0, at, :], do_ref[at, :]
        scores = masked(nt(k_ref[0, :end, :], queries) * SCALE, top)
        probs = jnp.exp(scores - lse_ref[0, block : block + 1, :])
        grad_probs = nt(v_ref[0, :end, :], grads)
        weighted = probs * grad_probs
        delta = jnp.sum(weighted, axis=0, keepdims=True)
        grad_scores = (probs * (grad_probs - delta)).astype(jnp.bfloat16)
        dv = nn(probs.astype(jnp.bfloat16), grads)
        dk = nn(grad_scores, queries)
        if block == 3:
            dv_ref[...] = dv
            dk_ref[...] = dk
        else:
            dv_ref[:end, :] += dv
            dk_ref[:end, :] += dk
        dq_ref[at, :] = nn(key_t[:, :end], grad_scores).T

    def low(value):
        return value.astype(jnp.bfloat16).astype(jnp.float32)

    for g in range(count):

        @pl.when(heads == g)
        def _(g=g):
            for part, block in enumerate(BLOCKS):
                here = pl.ds(part * span, span)
                there = pl.ds(block * span, span)
                cos, sin = cos_ref[here, :], -sin_ref[here, :]
                both = [
                    rope(low(dq_ref[pl.ds((2 * block + a) * span, span), :] * SCALE), cos, sin)
                    for a in range(2)
                ]
                out_ref[here, 2 * g * HD : (2 * g + 2) * HD] = jnp.concatenate(
                    both, axis=1
                ).astype(jnp.bfloat16)
                at = (2 * count + g) * HD
                out_ref[here, at : at + HD] = rope(
                    low(dk_ref[there, :] * SCALE), cos, sin
                ).astype(jnp.bfloat16)
                at = (3 * count + g) * HD
                out_ref[here, at : at + HD] = dv_ref[there, :].astype(jnp.bfloat16)


def attend_backward(q, k, v, lse, grad_mixed, cos, sin):
    groups, rows, _ = k.shape
    span = rows // 4
    whole = lambda shape: pl.BlockSpec(shape, lambda g: (0,) * len(shape))
    each = lambda shape: pl.BlockSpec((1,) + shape, lambda g: (g,) + (0,) * len(shape))
    return pl.pallas_call(
        backward_kernel,
        grid=(groups,),
        in_specs=[
            each((2 * rows, HD)),
            each((rows, HD)),
            each((rows, HD)),
            each((4, 2 * span)),
            whole(grad_mixed.shape),
            whole(cos.shape),
            whole(sin.shape),
        ],
        out_specs=whole((rows, 4 * groups * HD)),
        out_shape=jax.ShapeDtypeStruct((rows, 4 * groups * HD), jnp.bfloat16),
        scratch_shapes=[
            pltpu.VMEM((2 * rows, HD), jnp.bfloat16),
            pltpu.VMEM((2 * rows, HD), jnp.float32),
            pltpu.VMEM((rows, HD), jnp.float32),
            pltpu.VMEM((rows, HD), jnp.float32),
        ],
        compiler_params=pltpu.CompilerParams(vmem_limit_bytes=48 * 1024 * 1024),
        cost_estimate=SMALL,
        name="attention_backward",
    )(q, k, v, lse, grad_mixed, cos, sin)


def other_core(value):
    return lax.ppermute(value, "seq", CORE_SWAP)


def other_y(value):
    return lax.ppermute(value, "seq", Y_SWAP)


def tie(value, *after):
    flat = value.reshape(-1, value.shape[-1])
    spec = pl.BlockSpec(memory_space=pltpu.HBM)
    tied = pl.pallas_call(
        lambda *refs: None,
        in_specs=[spec] * (1 + len(after)),
        out_specs=spec,
        out_shape=jax.ShapeDtypeStruct(flat.shape, flat.dtype),
        input_output_aliases={0: 0},
        name="tie",
    )(flat, *after)
    return tied.reshape(value.shape)


def gather_dp(piece):
    return lax.all_gather(piece, "dp", axis=0, tiled=True)


def dp_bits():
    count = lax.axis_size("dp").bit_length() - 1
    return [0] + list(range(count - 1, 0, -1))


def dp_swap(value, bit):
    size = lax.axis_size("dp")
    return lax.ppermute(value, "dp", [(d, d ^ (1 << bit)) for d in range(size)])


def by_bits(full):
    size = lax.axis_size("dp")
    count = size.bit_length() - 1
    return full.reshape((2,) * count + (full.shape[0] // size,) + full.shape[1:])


def halve(value, bit, left):
    axis = sorted(left, reverse=True).index(bit)
    own = (lax.axis_index("dp") >> bit) & 1
    kept = lax.dynamic_index_in_dim(value, own, axis, keepdims=False)
    sent = lax.dynamic_index_in_dim(value, 1 - own, axis, keepdims=False)
    return kept + dp_swap(sent, bit)


def halve_tied(value, bit, left, before):
    axis = sorted(left, reverse=True).index(bit)
    own = (lax.axis_index("dp") >> bit) & 1
    kept = lax.dynamic_index_in_dim(value, own, axis, keepdims=False)
    sent = lax.dynamic_index_in_dim(value, 1 - own, axis, keepdims=False)
    if before is not None:
        sent = tie(sent, before)
    got = dp_swap(sent, bit)
    return kept + got, got


def halve_all(value, order):
    for step, bit in enumerate(order):
        value = halve(value, bit, order[step:])
    return value


def scatter_dp(full):
    order = dp_bits()
    return halve_all(by_bits(full), order)


def double_dp(piece):
    order = dp_bits()[::-1]
    value = piece
    done = []
    for bit in order:
        got = dp_swap(value, bit)
        done.append(bit)
        axis = sorted(done, reverse=True).index(bit)
        own = (lax.axis_index("dp") >> bit) & 1
        value = pair(own, jnp.expand_dims(value, axis), jnp.expand_dims(got, axis), axis)
    return value.reshape((-1,) + piece.shape[1:])


def dot(left, right):
    return jnp.dot(left, right, preferred_element_type=jnp.float32)


def dot_t(left, right):
    return lax.dot_general(
        left, right, (((1,), (1,)), ((), ())), preferred_element_type=jnp.float32
    )


def tdot(left, right):
    out = lax.dot_general(
        left, right, (((0,), (0,)), ((), ())), preferred_element_type=jnp.float32
    ).astype(jnp.bfloat16)
    return layout.with_layout_constraint(out, layout.Layout(major_to_minor=(0, 1)))


def pair(flag, mine, other, axis=0):
    return jnp.where(
        flag == 0,
        jnp.concatenate([mine, other], axis=axis),
        jnp.concatenate([other, mine], axis=axis),
    )


def norm_rows(stream, gain):
    inverse = lax.rsqrt(jnp.mean(stream * stream, axis=-1, keepdims=True) + EPSILON)
    normed = stream * inverse
    return (normed, inverse, (normed * gain).astype(jnp.bfloat16))


def norm_back(grad_out, normed, inverse, gain):
    gain_grad = jnp.sum(grad_out * normed, axis=0)
    scaled = grad_out * gain
    grad_in = inverse * (scaled - normed * jnp.mean(scaled * normed, axis=-1, keepdims=True))
    return (grad_in, gain_grad)


def mlp_back_kernel(*refs):
    grad_ref, input_t_ref, gate_ref, up_ref, gate_w_ref, up_w_ref, down_w_ref = refs[:7]
    before = refs[7:-4]
    total_ref, *out_refs = refs[-4:]
    step = pl.program_id(0)
    pieces = []
    size = gate_ref.shape[0] // 4
    for piece in range(4):
        rows = pl.ds(piece * size, size)
        gate, up = gate_ref[rows, :], up_ref[rows, :]
        grad_hidden = nt(grad_ref[rows, :], down_w_ref[...])
        sig = 1.0 / (1.0 + jnp.exp(-gate))
        swish = gate * sig
        grad_gate = grad_hidden * up * (sig + swish * (1.0 - sig))
        pieces.append(
            (
                grad_gate.astype(jnp.bfloat16),
                (grad_hidden * swish).astype(jnp.bfloat16),
                (swish * up).T.astype(jnp.bfloat16),
            )
        )
    grad_gate, grad_up, hidden_t = (
        jnp.concatenate(part, axis=axis) for part, axis in zip(zip(*pieces), (0, 0, 1))
    )
    term = nt(
        jnp.concatenate([grad_gate, grad_up], axis=1),
        jnp.concatenate([gate_w_ref[...], up_w_ref[...]], axis=1),
    )

    @pl.when(step == 0)
    def _():
        total_ref[...] = term

    @pl.when(step > 0)
    def _():
        total_ref[...] += term

    sums = [
        nn(input_t_ref[...], grad_gate),
        nn(input_t_ref[...], grad_up),
        nn(hidden_t, grad_ref[...]),
    ]
    for at, (out, value) in enumerate(zip(out_refs, sums)):
        if before:
            value = value + before[at][...].astype(jnp.float32)
        out[...] = value.astype(jnp.bfloat16)


def mlp_back(grad, input_t, gate_up, gate_up_w, down_w, before):
    tokens, features = grad.shape
    tile = 256
    width = down_w.shape[0]
    steps = width // tile

    def whole(shape):
        return pl.BlockSpec(shape, lambda t: (0, 0), pipeline_mode=pl.Buffered(1))

    def column(rows, first):
        return pl.BlockSpec((rows, tile), lambda t: (0, first + t))

    row = pl.BlockSpec((tile, features), lambda t: (t, 0))
    weight_specs = [column(features, 0), column(features, 0), row]
    return pl.pallas_call(
        mlp_back_kernel,
        grid=(steps,),
        in_specs=[
            whole(grad.shape),
            whole(input_t.shape),
            column(tokens, 0),
            column(tokens, steps),
            column(features, 0),
            column(features, steps),
            row,
            *(weight_specs if before else []),
        ],
        out_specs=[pl.BlockSpec((tokens, features), lambda t: (0, 0)), *weight_specs],
        out_shape=[
            jax.ShapeDtypeStruct((tokens, features), jnp.float32),
            jax.ShapeDtypeStruct((features, width), jnp.bfloat16),
            jax.ShapeDtypeStruct((features, width), jnp.bfloat16),
            jax.ShapeDtypeStruct((width, features), jnp.bfloat16),
        ],
        compiler_params=pltpu.CompilerParams(vmem_limit_bytes=60 * 1024 * 1024),
        cost_estimate=SMALL,
        name="mlp_backward",
    )(grad, input_t, gate_up, gate_up, gate_up_w, gate_up_w, down_w, *before)


def assemble_kernel(part, cuts, place_ref, *refs):
    groups = [refs[4 * i : 4 * i + 4] for i in range(len(cuts))]
    outs = refs[-cuts_outputs(cuts) :]
    for place in range(4):

        @pl.when(place_ref[0] == place)
        def _(place=place):
            for pieces, parts in zip(groups, cuts):
                by_place = {place ^ swap: ref for swap, ref in zip((0, 2, 1, 3), pieces)}
                for kind, at, size, out in parts:
                    here = slice(at, at + size)
                    if kind == "columns":
                        for quarter in range(4):
                            for start in range(0, size, part):
                                to = 4 * start + quarter * part
                                value = by_place[quarter][:, at + start : at + start + part]
                                outs[out][0, :, to : to + part] = value.astype(jnp.float32)
                    elif kind == "rows":
                        for quarter in range(4):
                            value = by_place[quarter][:, here].astype(jnp.float32)
                            outs[out][0, quarter * part : (quarter + 1) * part, :] = value
                    elif kind in ("blocks", "gains"):
                        for half in range(2):
                            values = [by_place[2 * half + core][:, here] for core in range(2)]
                            values = [value.astype(jnp.float32) for value in values]
                            count = values[0].shape[0]
                            to = slice(half * count, (half + 1) * count)
                            if kind == "gains":
                                outs[out][0, to, :] = values[0] + values[1]
                            else:
                                outs[out][0, to, :size] = values[0]
                                outs[out][0, to, size:] = values[1]
                    else:
                        halves = [
                            by_place[half][:, here].astype(jnp.float32)
                            + by_place[half + 2][:, here].astype(jnp.float32)
                            for half in range(2)
                        ]
                        for half in range(2):
                            outs[out][0, :, half * size : (half + 1) * size] = halves[half]


def cuts_outputs(cuts):
    return 1 + max(out for parts in cuts for *_, out in parts)


def assemble(place, layer, groups, cuts, shapes, part, before):
    operands = [piece for group in groups for piece in group]
    in_specs = [pl.BlockSpec(memory_space=pltpu.SMEM)]
    in_specs += [pl.BlockSpec(piece.shape, lambda i: (0, 0)) for piece in operands]
    aliases = {}
    if before is not None:
        aliases = {1 + len(operands) + i: i for i in range(len(before))}
        operands += before
        in_specs += [pl.BlockSpec(memory_space=pl.ANY)] * len(before)
    return pl.pallas_call(
        functools.partial(assemble_kernel, part, cuts),
        grid=(1,),
        in_specs=in_specs,
        out_specs=[pl.BlockSpec((1,) + shape[1:], lambda i: (layer, 0, 0)) for shape in shapes],
        out_shape=[jax.ShapeDtypeStruct(shape, jnp.float32) for shape in shapes],
        input_output_aliases=aliases,
        compiler_params=pltpu.CompilerParams(vmem_limit_bytes=60 * 1024 * 1024),
        name="assemble",
    )(place, *operands)


def body(
    tokens, cotangent, attn_norm, w_query, w_key, w_value, w_out, mlp_norm, w_gate, w_up, w_down
):
    dp_size = lax.axis_size("dp")
    index = lax.axis_index("seq")
    core = index % 2
    side = index // 2
    _, span, features = tokens.shape
    layers = w_query.shape[0]
    rows = w_query.shape[1]
    q_half = w_query.shape[2] // 2
    k_half = w_key.shape[2] // 2
    ff = w_gate.shape[2]
    part = ff // (4 * dp_size)
    ff_quarter = ff // 4
    out_half = features // 2
    heads = q_half // HD
    kv_heads = k_half // HD
    mine_rows = 2 * span
    length = 4 * span

    def regroup(*blocks):
        kept = [lax.dynamic_index_in_dim(block, side, 0, keepdims=False) for block in blocks]
        sent = [lax.dynamic_index_in_dim(block, 1 - side, 0, keepdims=False) for block in blocks]
        got = other_y(jnp.stack(sent))
        return [pair(side, mine, other) for mine, other in zip(kept, got)], got

    def swapped(block):
        halves = block.reshape(2, span, features)
        sent = lax.dynamic_index_in_dim(halves, 1 - side, 0, keepdims=False)
        return other_y(sent.astype(jnp.bfloat16))

    def ungroup(block, got):
        halves = block.reshape(2, span, features)
        kept = lax.dynamic_index_in_dim(halves, side, 0, keepdims=False)
        return pair(side, kept[None], got[None].astype(kept.dtype))

    def both_cores(value):
        return pair(core, value, other_core(value))

    def own_rows(total):
        kept = lax.dynamic_slice_in_dim(total, core * mine_rows, mine_rows, 0)
        sent = lax.dynamic_slice_in_dim(total, (1 - core) * mine_rows, mine_rows, 0)
        got = other_core(sent.astype(jnp.bfloat16))
        return kept + got.astype(jnp.float32)

    block_order = jnp.array([0, 2, 1, 3], jnp.int32)
    positions = (block_order[:, None] * span + jnp.arange(span)[None, :]).reshape(-1)
    middle = HD // 2
    frequency = ROPE_BASE ** (-jnp.arange(middle, dtype=jnp.float32) / middle)
    angles = positions.astype(jnp.float32)[:, None] * frequency[None, :]
    cosine = jnp.tile(jnp.cos(angles), (1, 2))
    sine = jnp.concatenate([-jnp.sin(angles), jnp.sin(angles)], axis=1)

    qkv_width = q_half + 2 * k_half
    gain_cols = jnp.pad(
        jnp.stack([attn_norm, mlp_norm]).reshape(2 * layers, rows).T,
        ((0, 0), (0, 128 - 2 * layers)),
    )

    (stream, grad), came = regroup(tokens, cotangent)
    came = came.reshape(-1, features)

    def quarter(weight):
        cut = weight.reshape(rows, dp_size, 4, part)
        return lax.dynamic_index_in_dim(cut, index, 2, keepdims=False).reshape(rows, ff_quarter)

    def attention_local(layer):
        local = [
            lax.dynamic_slice_in_dim(w_query[layer], core * q_half, q_half, 1),
            lax.dynamic_slice_in_dim(w_key[layer], core * k_half, k_half, 1),
            lax.dynamic_slice_in_dim(w_value[layer], core * k_half, k_half, 1),
            lax.dynamic_slice_in_dim(w_out[layer], core * out_half, out_half, 1),
        ]
        if layer == 0:
            local.insert(3, gain_cols)
        local = jnp.concatenate(local, axis=1).reshape(2, rows // 2, -1)
        return lax.dynamic_index_in_dim(local, side, 0, keepdims=False)

    gate_up_locals = [
        jnp.concatenate([quarter(w_gate[layer]), quarter(w_up[layer])], axis=1)
        for layer in range(layers)
    ]
    down_locals = [
        lax.dynamic_slice_in_dim(w_down[layer], index * part, part, 0) for layer in range(layers)
    ]
    halves = [gather_dp(attention_local(0))]
    for layer in range(1, layers):
        halves.append(gather_dp(tie(attention_local(layer), came, *gate_up_locals, *down_locals)))

    def joined(near, far):
        near, far = (half.reshape(dp_size, 1, rows // 2, -1) for half in (near, far))
        return pair(side, near, far, axis=1).reshape(features, -1)

    firsts = halves[0].shape[1] - out_half
    far_qkv = other_y(halves[0][:, :firsts])
    far_out = other_y(tie(halves[0][:, firsts:], far_qkv))
    last_far = far_out
    fars = []
    for layer in range(1, layers):
        last_far = other_y(tie(halves[layer], last_far))
        fars.append(last_far)
    far_qkv = tie(far_qkv, *halves[1:])
    first_qkv = joined(halves[0][:, :firsts], far_qkv)
    attention_weights = [(first_qkv[:, :qkv_width], joined(halves[0][:, firsts:], far_out))]
    for near, far in zip(halves[1:], fars):
        joint = joined(near, far)
        attention_weights.append((joint[:, :qkv_width], joint[:, qkv_width:]))
    all_weights = []
    for layer in range(layers):
        gate_up = gate_up_locals[layer]
        gate_up = gather_dp(tie(gate_up, halves[1]) if layer == 0 else gate_up)
        down = gather_dp(down_locals[layer])
        qkv, out_cols = attention_weights[layer]
        kept = lax.dynamic_slice_in_dim(out_cols, core * q_half, q_half, 0)
        sent = lax.dynamic_slice_in_dim(out_cols, (1 - core) * q_half, q_half, 0)
        out = pair(core, kept, other_core(sent), axis=1)
        all_weights.append((qkv, out, gate_up, down))
    gains = first_qkv[:, qkv_width : qkv_width + 2 * layers].T.astype(jnp.float32)
    gains = gains.reshape(2, layers, features)

    def forward(stream, weights, gain_one, gain_two, ready, last):
        qkv_w, out_w, gate_up_w, down_w = weights
        normed_one, inverse_one, input_one = norm_rows(stream, gain_one)
        full_one = both_cores(input_one)
        raw = dot(full_one, qkv_w)
        mixed, *attended = attend_forward(raw, cosine, sine)
        mixed = tie(mixed, ready)
        stream_two = stream + own_rows(dot(mixed, out_w))
        normed_two, inverse_two, input_two = norm_rows(stream_two, gain_two)
        def turned(inputs):
            return layout.with_layout_constraint(
                inputs.T, layout.Layout(major_to_minor=(0, 1))
            )

        def hidden_of(gate_up):
            gate, up = gate_up[:, :ff_quarter], gate_up[:, ff_quarter:]
            return (jax.nn.silu(gate) * up).astype(jnp.bfloat16)

        far = other_y(input_two)
        near_in = both_cores(input_two)
        near_turned = turned(near_in)
        near_gate_up = dot(near_in, gate_up_w)
        far_in = both_cores(tie(far, near_gate_up, near_turned))
        far_gate_up = dot(far_in, gate_up_w)
        far_turned = turned(far_in)

        def down_dots(after):
            pieces = [near_gate_up, far_gate_up]
            if after is not None:
                pieces = [tie(piece, after) for piece in pieces]
            return [dot(hidden_of(piece), down_w) for piece in pieces]

        def finish(totals, meanwhile):
            near_total, far_total = totals
            far_rows = own_rows(far_total).astype(jnp.bfloat16)
            far = tie(other_y(far_rows), meanwhile)
            near = own_rows(tie(near_total, far_total))
            return stream_two + (near + far.astype(jnp.float32))

        result = (down_dots, finish) if last else finish(down_dots(None), far_turned)
        kept_mlp = [(near_turned, near_gate_up), (far_turned, far_gate_up)]
        saved = (
            normed_one,
            inverse_one,
            full_one,
            attended,
            mixed,
            normed_two,
            inverse_two,
            kept_mlp,
        )
        return result, saved

    def backward(grad, saved, weights, gain_one, gain_two, far, fill):
        (
            normed_one,
            inverse_one,
            full_one,
            attended,
            mixed,
            normed_two,
            inverse_two,
            kept_mlp,
        ) = saved
        qkv_w, out_w, gate_up_w, down_w = weights
        grad_low = grad.astype(jnp.bfloat16)
        late = None
        if fill is not None:
            down_dots, finish = fill
            totals = down_dots(grad_low)
            far = tie(other_y(grad_low), *totals)
        far, *mlp_grads = mlp_back(both_cores(far), *kept_mlp[1], gate_up_w, down_w, [])
        far_rows = own_rows(far).astype(jnp.bfloat16)
        far = other_y(far_rows)
        if fill is not None:
            late = finish(totals, far)
        near = tie(both_cores(grad_low), far_rows)
        near, *mlp_grads = mlp_back(near, *kept_mlp[0], gate_up_w, down_w, mlp_grads)
        grad_two = own_rows(tie(near, far)) + far.astype(jnp.float32)
        norm_two_in, gain_two_g = norm_back(grad_two, normed_two, inverse_two, gain_two)
        grad_mid = grad + norm_two_in
        mid_full = both_cores(grad_mid.astype(jnp.bfloat16))
        grad_out_w = tdot(mixed, mid_full)
        grad_mixed = dot_t(mid_full, out_w).astype(jnp.bfloat16)
        if late is not None:
            got = swapped(late)
            grad_mixed = tie(grad_mixed, got, grad_out_w)
            late = (late, got)
        grad_qkv = attend_backward(*attended, grad_mixed, cosine, sine)
        grad_qkv_w = tdot(full_one, grad_qkv)
        low = grad_qkv if fill is None else tie(grad_qkv, grad_qkv_w)
        grad_one = own_rows(dot_t(low, qkv_w))
        norm_one_in, gain_one_g = norm_back(grad_one, normed_one, inverse_one, gain_one)
        grad = grad_mid + norm_one_in
        points = (mid_full, grad_qkv, grad_one)
        parts = (mlp_grads, grad_out_w, grad_qkv_w, gain_one_g, gain_two_g)
        return grad, parts, points, late

    def four(piece):
        got = other_y(piece)
        return [piece, got, other_core(piece), other_core(got)]

    def reduce_last(grads, out_grad, qkv_grad, points, earlier, grad):
        _, after_attention, after_all = points
        gate, up, down = grads
        order = dp_bits()
        last = {"x": None, "z": None, "any": after_attention}

        def send(value, step, link):
            value = by_bits(value) if step == 0 else value
            left = order[step:]
            axis = sorted(left, reverse=True).index(left[0])
            own = (lax.axis_index("dp") >> left[0]) & 1
            kept = lax.dynamic_index_in_dim(value, own, axis, keepdims=False)
            sent = lax.dynamic_index_in_dim(value, 1 - own, axis, keepdims=False)
            if link and last[link] is not None:
                sent = tie(sent, last[link])
            got = dp_swap(sent, left[0])
            if link:
                last[link] = got
            return kept, got

        def take(got):
            got = tie(got, last["any"])
            last["any"] = got
            return got

        def add(pending):
            return pending[0] + take(pending[1])

        def four_taken(piece):
            got = take(other_y(piece))
            return [piece, got, other_core(piece), other_core(got)]

        def finish(value):
            for step in range(2, len(order)):
                value = add(send(value, step, None))
            return value

        def sides(value):
            cut = value.reshape(dp_size, 2, rows // 2, -1)
            kept = lax.dynamic_index_in_dim(cut, side, 1, keepdims=False)
            sent = lax.dynamic_index_in_dim(cut, 1 - side, 1, keepdims=False)
            shape = (features // 2, -1)
            return kept.reshape(shape), sent.reshape(shape)

        gate_up = send(jnp.concatenate([gate, up], axis=1), 0, "x")
        out_near, sent = sides(out_grad)
        out_far = other_y(sent)
        qkv_near, sent = sides(qkv_grad)
        qkv_far = other_y(tie(sent, out_far))
        gate_up = send(add(gate_up), 1, "z")
        last["x"] = tie(after_attention, last["x"].reshape(-1, last["x"].shape[-1]))
        down = send(down, 0, "x")
        down = send(add(down), 1, "z")
        out = send(out_near + take(out_far), 0, "x")
        out = send(add(out), 1, "z")
        gate_up = finish(add(gate_up))
        qkv = send(qkv_near + take(qkv_far), 0, "x")
        down = finish(add(down))
        out = finish(add(out))
        qkv = send(add(qkv), 1, "z")
        earlier = [[four_taken(piece) for piece in pieces] for pieces in earlier]
        gate_up = four_taken(gate_up)
        down = four_taken(down)
        got_grad = take(swapped(grad))
        qkv = finish(add(qkv))
        joint = jnp.concatenate([out, qkv], axis=1)
        cuts = [
            [("columns", 0, ff_quarter, 0), ("columns", ff_quarter, ff_quarter, 1)],
            attention_cuts(0, "blocks") + [("gains", joint.shape[1] - 128, 128, 7)],
            [("rows", 0, features, 2)],
        ]
        return ([gate_up, four(joint), down], cuts), earlier, got_grad

    def attention_cuts(at, kind="halves"):
        sizes = (out_half, q_half, k_half, k_half)
        firsts = [at + sum(sizes[:i]) for i in range(4)]
        return [(kind, first, size, 3 + i) for i, (first, size) in enumerate(zip(firsts, sizes))]

    def reduce_first(grads, out_grad, qkv_grad, points):
        gate, up, down = grads
        down = lax.psum_scatter(down, "dp", scatter_dimension=0, tiled=True)
        joint = jnp.concatenate([gate, up, out_grad, qkv_grad], axis=1)
        piece = lax.psum_scatter(joint, "dp", scatter_dimension=0, tiled=True)
        cuts = [
            [("columns", 0, ff_quarter, 0), ("columns", ff_quarter, ff_quarter, 1)]
            + attention_cuts(2 * ff_quarter),
            [("rows", 0, features, 2)],
        ]
        return [piece, down], cuts

    def columns_of_core(grad):
        kept = lax.dynamic_slice_in_dim(grad, core * out_half, out_half, 1)
        sent = lax.dynamic_slice_in_dim(grad, (1 - core) * out_half, out_half, 1)
        return pair(core, kept, other_core(sent), axis=0)

    stream, grad = stream.astype(jnp.float32), grad.astype(jnp.float32)
    far_cotangent = other_y(grad.astype(jnp.bfloat16))
    all_saved = []
    for layer in range(layers):
        ready = far_cotangent if layer == layers - 1 else fars[layer]
        stream, saved = forward(
            stream, all_weights[layer], gains[0, layer], gains[1, layer], ready, layer == layers - 1
        )
        all_saved.append(saved)
    reduced = [None] * layers
    gain_grads = []
    for layer in reversed(range(layers)):
        grad, (mlp_g, out_g, qkv_g, one_g, two_g), points, late = backward(
            grad,
            all_saved[layer],
            all_weights[layer],
            gains[0, layer],
            gains[1, layer],
            far_cotangent if layer == layers - 1 else None,
            stream if layer == 0 else None,
        )
        gain_grads = [one_g, two_g] + gain_grads
        out_g = columns_of_core(out_g)
        if layer > 0:
            reduced[layer] = reduce_first(mlp_g, out_g, qkv_g, points)
        else:
            extra = jnp.stack(gain_grads, axis=1)
            extra = jnp.pad(extra, ((0, 0), (0, 128 - extra.shape[1])))
            qkv_g = jnp.concatenate([qkv_g, extra.astype(jnp.bfloat16)], axis=1)
            earlier = [reduced[at][0] for at in range(1, layers)]
            reduced[0], earlier, got = reduce_last(
                mlp_g, out_g, qkv_g, points, earlier, grad
            )
    output = ungroup(*late).astype(jnp.bfloat16)
    d_tokens = ungroup(grad, got)
    for layer in range(1, layers):
        reduced[layer] = earlier[layer - 1], reduced[layer][1]
    shapes = [(layers, rows, ff)] * 2 + [(layers, 4 * part, features)]
    shapes += [(layers, rows, 2 * size) for size in (out_half, q_half, k_half, k_half)]
    place = index.astype(jnp.int32).reshape(1)
    outs = None
    for layer in range(layers - 1, 0, -1):
        outs = assemble(place, layer, *reduced[layer], shapes, part, outs)
    outs = assemble(place, 0, *reduced[0], shapes + [(1, rows, 128)], part, outs)
    gate_out, up_out, down_out, out_out, query_out, key_out, value_out, gain_out = outs
    gain_out = gain_out[0, :, : 2 * layers].T.reshape(layers, 2, rows)
    return (
        output,
        d_tokens,
        gain_out[:, 0],
        query_out,
        key_out,
        value_out,
        out_out,
        gain_out[:, 1],
        gate_out,
        up_out,
        down_out,
    )


def solution(mesh):
    in_specs = (
        P("dp", "seq", None),
        P("dp", "seq", None),
        P(None, "dp"),
        P(None, "dp", None),
        P(None, "dp", None),
        P(None, "dp", None),
        P(None, "dp", None),
        P(None, "dp"),
        P(None, "dp", None),
        P(None, "dp", None),
        P(None, "dp", None),
    )
    return jax.shard_map(
        body, mesh=mesh, in_specs=in_specs, out_specs=in_specs, check_vma=False
    )
```
